256 devices in a mesh: lev: 4 (over z_lo, core), row: 64 (over x, y, z_hi).
Axes of the slice: x: 4, y: 4, z: 8 (z_hi: 4, z_lo: 2; z = z_hi * 2 + z_lo), core: 2. Of those that a mesh axis runs over, the one named last changes fastest.
Arguments:
- wind_east: float32 [16, 1024, 1024], P('lev', 'row'), may hold values from -3 to 3
- wind_north: float32 [16, 1024, 1024], P('lev', 'row'), may hold values from -3 to 3
- thickness: float32 [16, 1024, 1024], P('lev', 'row'), may hold values from 0.5 to 2
- tracer_one: float32 [16, 1024, 1024], P('lev', 'row'), may hold values from 0 to 1
- tracer_two: float32 [16, 1024, 1024], P('lev', 'row'), may hold values from 0.1 to 1
- theta_step: float32 [16], replicated, may hold values from 0.5 to 2
- surface_geopot: float32 [1024, 1024], P('row'), may hold values from -12 to 12
- map_factor: float32 [1024, 1024], P('row'), may hold values from 0.5 to 2
- active_layers: int32 [1024, 1024], P('row'), may hold values from 8 to 16
Outputs:
- east_out: float32 [16, 1024, 1024], P('lev', 'row')
- north_out: float32 [16, 1024, 1024], P('lev', 'row')
- thickness_out: float32 [16, 1024, 1024], P('lev', 'row')
- tracer_one_out: float32 [16, 1024, 1024], P('lev', 'row')
- tracer_two_out: float32 [16, 1024, 1024], P('lev', 'row')
The draws below stay inside these ranges and needn't reach their ends.
Inputs may be any that keep to these rules, and one draw needn't show every extreme that they name: Layers k with k >= active_layers of their column are below ground and keep their values.
All inputs are finite; a program needn't handle non-finite values.
Results may differ from the reference program's by a relative error of at most 0.00002.
Values sent between devices are 32-bit elements; how exact they have to be, the bound alone decides.
A program may use at most 64 MiB of HBM per device.

```python
import math
import jax
import jax.numpy as jnp

NY = 1024
OUTER = 2
L = 16
NX = 1024


def plant(entries, own_key, low, top_value):
    longest = entries.shape.index(max(entries.shape))
    spots = []
    for shift in (0, 1):
        where = [jax.random.randint(jax.random.fold_in(own_key, axis), (), 0, length) for axis, length in enumerate(entries.shape)]
        where[longest] = (where[longest] + shift) % entries.shape[longest]
        spots.append(tuple(where))
    return entries.at[spots[0]].set(low).at[spots[1]].set(top_value)


def shard_levels(stream_key, extent, pieces, smallest, high):
    gain = 1.0
    for dim, parts in pieces:
        heights = jax.random.uniform(jax.random.fold_in(jax.random.fold_in(stream_key, 6), dim), (parts,), jnp.float32, smallest / len(pieces), high / len(pieces))
        gain = gain * jnp.repeat(jnp.exp(heights), extent[dim] // parts).reshape((-1,) + (1,) * (len(extent) - 1 - dim))
    return gain


def scatter_about(key, dims, width, bound, pieces=(), held_as=jnp.bfloat16):
    level = shard_levels(key, dims, pieces, -0.22, 0.18) if pieces else 1.0
    drawn = jax.random.normal(key, dims, jnp.float32) * width * level
    return jnp.minimum(jnp.maximum(drawn, -bound), bound).astype(held_as)


def setup_inputs(seed: int = 0) -> dict:
    keys = jax.random.split(jax.random.key(seed), 10)
    wind_east = scatter_about(keys[0], (L, NX, NY), 0.5, 3.0, ((0, 4), (1, 64)), jnp.float32)
    wind_north = scatter_about(keys[1], (L, NX, NY), 0.5, 3.0, ((0, 4), (1, 64)), jnp.float32)
    thickness = jnp.clip(jnp.exp(math.log(2.0) - 1.3862944 * jax.random.uniform(keys[2], (L, NX, NY), jnp.float32) ** shard_levels(keys[2], (L, NX, NY), ((0, 4), (1, 64)), -0.2, 0.2)), 0.5, 2.0)
    tracer_one = jnp.clip(1.0 * jax.random.uniform(keys[3], (L, NX, NY), jnp.float32) ** shard_levels(keys[3], (L, NX, NY), ((0, 4), (1, 64)), -0.2, 0.2), 0.0, 1.0)
    tracer_two = jnp.clip(jnp.exp(math.log(1.0) - 2.3025851 * jax.random.uniform(keys[4], (L, NX, NY), jnp.float32) ** shard_levels(keys[4], (L, NX, NY), ((0, 4), (1, 64)), -0.2, 0.2)), 0.1, 1.0)
    theta_step = jnp.clip(jnp.exp(jax.random.uniform(keys[5], (L,), jnp.float32, math.log(0.5), math.log(2.0))), 0.5, 2.0)
    surface_geopot = scatter_about(keys[6], (NX, NY), 2.0, 12.0, ((0, 64),), jnp.float32)
    map_factor = jnp.clip(jnp.exp(math.log(2.0) - 1.3862944 * jax.random.uniform(keys[7], (NX, NY), jnp.float32) ** shard_levels(keys[7], (NX, NY), ((0, 64),), -0.2, 0.2)), 0.5, 2.0)
    active_layers = plant(jax.random.randint(keys[8], (NX, NY), L // 2, L + 1), jax.random.fold_in(keys[8], 1), L // 2, L).astype(jnp.int32)
    return dict(wind_east=wind_east, wind_north=wind_north, thickness=thickness, tracer_one=tracer_one, tracer_two=tracer_two, theta_step=theta_step, surface_geopot=surface_geopot, map_factor=map_factor, active_layers=active_layers)


time_step = 0.05
top_pressure = 0.1
exner_power = 2.0 / 7.0


def potential_field(mass_field, theta_step, geopot):
    levels = mass_field.shape[0]
    pressure = top_pressure + jnp.cumsum(jnp.abs(mass_field), axis=0) / levels
    weighted = theta_step[:, None, None] * pressure ** exner_power
    summed = jnp.flip(jnp.cumsum(jnp.flip(weighted, 0), axis=0), 0)
    return geopot[None] + summed


def row_diff(values):
    return (jnp.roll(values, -1, 1) - jnp.roll(values, 1, 1)) * 0.5


def column_diff(values):
    padded = jnp.pad(values, ((0, 0), (0, 0), (1, 1)))
    return (padded[:, :, 2:] - padded[:, :, :-2]) * 0.5


def edge_diff(values):
    padded = jnp.pad(values, ((0, 0), (0, 0), (1, 1)), mode="edge")
    return (padded[:, :, 2:] - padded[:, :, :-2]) * 0.5


def tendency(fields, potential, metric, active, coriolis):
    east_mid, north_mid, mass_layer, tracer_first, tracer_last = fields[0], fields[1], fields[2], fields[3], fields[4]
    metric_mid = metric[None]
    flux_east = mass_layer * east_mid / metric_mid
    flux_north = mass_layer * north_mid / metric_mid
    d_mass = -(metric_mid * metric_mid) * (row_diff(flux_east) + column_diff(flux_north))

    def carried(values):
        return -metric_mid * (east_mid * row_diff(values) + north_mid * column_diff(values))

    d_east = carried(east_mid) + coriolis * north_mid - metric_mid * row_diff(potential)
    d_north = carried(north_mid) - coriolis * east_mid - metric_mid * edge_diff(potential)
    return jnp.stack([d_east, d_north, d_mass, carried(tracer_first), carried(tracer_last)]) * active[None]


def reference(wind_east, wind_north, thickness, tracer_one, tracer_two, theta_step, surface_geopot, map_factor, active_layers):
    levels = thickness.shape[0]
    columns = thickness.shape[2]
    layer_index = jnp.arange(levels, dtype=jnp.int32)[:, None, None]
    active = (layer_index < active_layers[None]).astype(jnp.float32)
    coriolis = 0.5 + jnp.arange(columns, dtype=jnp.float32)[None] / columns
    fields = jnp.stack([wind_east, wind_north, thickness, tracer_one, tracer_two])
    for outer_step in range(OUTER):
        potential = potential_field(fields[2], theta_step, surface_geopot)
        current = fields
        for fraction in (1.0 / 3.0, 0.5, 1.0):
            current = fields + (time_step * fraction) * tendency(current, potential, map_factor, active, coriolis)
        fields = current
    return fields[0], fields[1], fields[2], fields[3], fields[4]
```

```python
import functools

import jax
import jax.numpy as jnp
from jax import lax
from jax.experimental import pallas as pl
from jax.experimental.pallas import tpu as pltpu
from jax.sharding import PartitionSpec as P

OUTER = 2
SECTIONS = (1.0 / 3.0, 0.5, 1.0)

time_step = 0.05
top_pressure = 0.1
exner_power = 2.0 / 7.0

MESH = pl.DeviceIdType.MESH
VMEM = pltpu.VMEM

HALO = 3
OWN = 12
DEPTH = 40
LANES = 128
SUB = 8

TOTAL, PAIR, PAIR_UP, PAIR_DN, TOTAL_UP, TOTAL_DN = range(6)
EXNER, BELOW, BELOW_UP, BELOW_DN, EXNER_UP, EXNER_DN = range(6, 12)
MASS_UP, MASS_DN, WIND_UP, WIND_DN, TRACE_UP, TRACE_DN, PLANE_UP, PLANE_DN = range(12, 20)
MESSAGES = 20


def column_gap(a, edge=False):
    lane = lax.broadcasted_iota(jnp.int32, (1,) + a.shape[1:], 2)
    low, high = (a[:1], a[-1:]) if edge else (jnp.zeros_like(a[:1]), jnp.zeros_like(a[:1]))
    east = pltpu.roll(a, LANES - 1, 2)
    west = pltpu.roll(a, 1, 2)
    east = jnp.where(lane == LANES - 1, jnp.concatenate([east[1:], high], 0), east)
    west = jnp.where(lane == 0, jnp.concatenate([low, west[:-1]], 0), west)
    return east - west


def steps_kernel(
    levels,
    columns,
    row_devices,
    east_in,
    north_in,
    mass_in,
    one_in,
    two_in,
    theta,
    geopot_in,
    metric_in,
    active_in,
    east_out,
    north_out,
    mass_out,
    one_out,
    two_out,
    state,
    first,
    second,
    planes,
    active_raw,
    total,
    total_pair,
    pair,
    above,
    exner,
    exner_pair,
    low_pair,
    below,
    weight,
    potential,
    slope_x,
    slope_y,
    half_metric,
    half_square,
    spin,
    inverse,
    load_sem,
    send_sem,
    recv_sem,
):
    layers, blocks = state.shape[2], state.shape[3]
    lev, row = lax.axis_index("lev"), lax.axis_index("row")
    up_row = lax.rem(row + 1, row_devices)
    dn_row = lax.rem(row + row_devices - 1, row_devices)
    odd = lax.rem(lev, 2)
    core = (lev + 1 - 2 * odd, row)
    far_lev = lax.rem(lev + 2, 4)
    far, far_up, far_dn = (far_lev, row), (far_lev, up_row), (far_lev, dn_row)
    up, dn = (lev, up_row), (lev, dn_row)
    is_odd, is_even = odd == 1, odd == 0
    is_high, is_low = lev < 2, lev >= 2
    own = pl.ds(OWN, 2 * SUB)
    first_layer = lev * layers

    def load(slot, source, target):
        return [
            pltpu.make_async_copy(
                source(half), target(pl.ds(OWN + half * SUB, SUB)), load_sem.at[slot, half]
            )
            for half in range(2)
        ]

    def load_field(slot, ref, field):
        return load(slot, lambda half: ref.at[:, half], lambda rows: state.at[0, field, :, :, rows, :])

    loads_mass = load_field(0, mass_in, 2)
    loads_planes = (
        load(1, lambda half: metric_in.at[half], lambda rows: planes.at[0, :, rows, :])
        + load(2, lambda half: geopot_in.at[half], lambda rows: planes.at[1, :, rows, :])
        + load(3, lambda half: active_in.at[half], lambda rows: active_raw.at[:, rows, :])
    )
    loads_wind = load_field(4, east_in, 0) + load_field(5, north_in, 1)
    loads_trace = load_field(6, one_in, 3) + load_field(7, two_in, 4)
    for copy in loads_mass + loads_planes + loads_wind + loads_trace:
        copy.start()

    barrier = pltpu.get_barrier_semaphore()
    for device in (core, far, up, dn, far_up, far_dn):
        pl.semaphore_signal(barrier, inc=1, device_id=device, device_id_type=MESH)

    def message(outer, kind, source, target, device):
        return pltpu.make_async_remote_copy(
            src_ref=source,
            dst_ref=target,
            send_sem=send_sem.at[outer, kind],
            recv_sem=recv_sem.at[outer, kind],
            device_id=device,
            device_id_type=MESH,
        )

    edge_up = (pl.ds(OWN + 2 * SUB - HALO, HALO), pl.ds(OWN - HALO, HALO))
    edge_dn = (pl.ds(OWN, HALO), pl.ds(OWN + 2 * SUB, HALO))

    def edges(outer, kinds, ref, ref_to, to_up, to_dn):
        return [
            message(outer, kind, ref(rows[0]), ref_to(rows[1]), device)
            for kind, rows, device in zip(kinds, (edge_up, edge_dn), (to_up, to_dn))
        ]

    def plane_rows(ref, outer):
        return lambda rows: ref.at[outer, :, rows, :]

    def field_rows(outer, field, count):
        return lambda rows: state.at[outer, pl.ds(field, count), :, :, rows, :]

    def all_messages(outer):
        same = lambda kinds, ref: edges(outer, kinds, ref, ref, up, dn)
        msg = {}
        msg["total"] = [message(outer, TOTAL, total.at[outer, :, own, :], total_pair.at[outer, :, own, :], core)]
        msg["pair"] = [
            message(outer, PAIR, pair.at[outer, :, own, :], above.at[outer, :, own, :], far)
        ]
        msg["pair_edge"] = edges(
            outer, (PAIR_UP, PAIR_DN), plane_rows(pair, outer), plane_rows(above, outer), far_up, far_dn
        )
        msg["total_edge"] = same((TOTAL_UP, TOTAL_DN), plane_rows(total_pair, outer))
        msg["exner"] = [message(outer, EXNER, exner.at[outer, :, own, :], exner_pair.at[outer, :, own, :], core)]
        msg["below"] = [
            message(outer, BELOW, low_pair.at[outer, :, own, :], below.at[outer, :, own, :], far)
        ]
        msg["below_edge"] = edges(
            outer, (BELOW_UP, BELOW_DN), plane_rows(low_pair, outer), plane_rows(below, outer), far_up, far_dn
        )
        msg["exner_edge"] = same((EXNER_UP, EXNER_DN), plane_rows(exner_pair, outer))
        msg["mass"] = same((MASS_UP, MASS_DN), field_rows(outer, 2, 1))
        msg["wind"] = same((WIND_UP, WIND_DN), field_rows(outer, 0, 2))
        msg["trace"] = same((TRACE_UP, TRACE_DN), field_rows(outer, 3, 2))
        if outer == 0:
            msg["plane"] = same((PLANE_UP, PLANE_DN), lambda rows: planes.at[:, :, rows, :])
        return msg

    def start(copies):
        for copy in copies:
            copy.start()

    def arrive(copies):
        for copy in copies:
            copy.wait_recv()

    def sent(copies):
        for copy in copies:
            copy.wait_send()

    def tiles(count, body, unroll=1):
        def one(index, carry):
            body(index)
            return carry

        lax.fori_loop(0, count, one, 0, unroll=unroll)

    def sum_layers(outer):
        def body(tile):
            rows = pl.ds(OWN + SUB * tile, SUB)
            acc = jnp.abs(state[outer, 2, 0, :, rows, :])
            for layer in range(1, layers):
                acc = acc + jnp.abs(state[outer, 2, layer, :, rows, :])
            total[outer, :, rows, :] = acc

        tiles(2, body, 2)

    def add_planes(outer, out, one, other):
        def body(tile):
            rows = pl.ds(OWN + SUB * tile, SUB)
            out[outer, :, rows, :] = one[outer, :, rows, :] + other[outer, :, rows, :]

        tiles(2, body, 2)

    def weigh(outer, starts, keep_sum):
        base, stride = starts

        def body(tile):
            rows = pl.ds(base + stride * tile, SUB)
            running = jnp.where(is_odd, total_pair[outer, :, rows, :], 0.0) + jnp.where(
                is_low, above[outer, :, rows, :], 0.0
            )
            weighted = []
            for layer in range(layers):
                running = running + jnp.abs(state[outer, 2, layer, :, rows, :])
                pressure = top_pressure + running * (1.0 / levels)
                weighted.append(theta[first_layer + layer] * jnp.exp(exner_power * jnp.log(pressure)))
            acc = weighted[-1]
            weight[layers - 1, :, rows, :] = acc
            for layer in range(layers - 2, -1, -1):
                acc = acc + weighted[layer]
                weight[layer, :, rows, :] = acc
            if keep_sum:
                exner[outer, :, rows, :] = acc

        tiles(2, body)

    def coefficients(starts):
        base, stride = starts
        shape = (blocks, SUB, LANES)
        column = LANES * lax.broadcasted_iota(jnp.int32, shape, 0) + lax.broadcasted_iota(jnp.int32, shape, 2)
        coriolis = 0.5 + column.astype(jnp.float32) / columns

        def body(tile):
            rows = pl.ds(base + stride * tile, SUB)
            metric = planes[0, :, rows, :]
            count = planes[2, :, rows, :]
            inverse[:, rows, :] = 1.0 / metric
            half = 0.5 * metric
            square = half * metric
            for layer in range(layers):
                active = count > (first_layer + layer).astype(jnp.float32)
                half_metric[layer, :, rows, :] = jnp.where(active, half, 0.0)
                half_square[layer, :, rows, :] = jnp.where(active, square, 0.0)
                spin[layer, :, rows, :] = jnp.where(active, coriolis, 0.0)

        tiles(2, body)

    def montgomery(outer):
        def body(tile):
            rows = pl.ds(OWN - 4 + SUB * tile, SUB)
            rest = (
                planes[1, :, rows, :]
                + jnp.where(is_even, exner_pair[outer, :, rows, :], 0.0)
                + jnp.where(is_high, below[outer, :, rows, :], 0.0)
            )
            for layer in range(layers):
                potential[layer, :, rows, :] = rest + weight[layer, :, rows, :]

        tiles(3, body, 3)

        def slopes(index):
            layer, tile = index // 3, lax.rem(index, 3)
            base = OWN - 4 + SUB * tile
            rows = pl.ds(base, SUB)
            half = half_metric[layer, :, rows, :]
            slope_x[layer, :, rows, :] = half * (
                potential[layer, :, pl.ds(base + 1, SUB), :] - potential[layer, :, pl.ds(base - 1, SUB), :]
            )
            slope_y[layer, :, rows, :] = half * column_gap(potential[layer, :, rows, :], edge=True)

        tiles(3 * layers, slopes, 4)

    def section(outer, number, fields, results):
        count = 2 if number == 2 else 3
        begin = OWN if number == 2 else OWN - 4
        factor = time_step * SECTIONS[number]
        source = (state.at[outer], first, second)[number]

        def body(index):
            layer, tile = index // count, lax.rem(index, count)
            base = begin + SUB * tile

            def get(ref, field, shift=0):
                return ref[field, layer, :, pl.ds(base + shift, SUB), :]

            def plane(ref):
                return ref[layer, :, pl.ds(base, SUB), :]

            start_of = state.at[outer]
            half = plane(half_metric) * factor
            east, north = get(source, 0), get(source, 1)
            flow_x, flow_y = half * east, half * north

            def carried(field):
                middle = get(source, field)
                return flow_x * (get(source, field, 1) - get(source, field, -1)) + flow_y * column_gap(middle)

            if 0 in fields:
                turn = plane(spin) * factor
                results(0, layer, tile)[...] = (
                    get(start_of, 0) + (turn * north - plane(slope_x) * factor) - carried(0)
                )
                results(1, layer, tile)[...] = (
                    get(start_of, 1) - (turn * east + plane(slope_y) * factor) - carried(1)
                )

                def flux(shift):
                    return get(source, 2, shift) * get(source, 0, shift) * inverse[:, pl.ds(base + shift, SUB), :]

                across = get(source, 2) * north * plane_of(inverse, base)
                results(2, layer, tile)[...] = get(start_of, 2) - factor * plane(half_square) * (
                    (flux(1) - flux(-1)) + column_gap(across)
                )
            if 3 in fields:
                for field in (3, 4):
                    results(field, layer, tile)[...] = get(start_of, field) - carried(field)

        tiles(count * layers, body, 4)

    def plane_of(ref, base):
        return ref[:, pl.ds(base, SUB), :]

    outputs = (east_out, north_out, mass_out, one_out, two_out)

    def results_of(outer, number):
        if number < 2:
            ref = (first, second)[number]
            return lambda field, layer, tile: ref.at[field, layer, :, pl.ds(OWN - 4 + SUB * tile, SUB), :]
        if outer + 1 < OUTER:
            return lambda field, layer, tile: state.at[outer + 1, field, layer, :, pl.ds(OWN + SUB * tile, SUB), :]
        return lambda field, layer, tile: outputs[field].at[layer, :, pl.ds(SUB * tile, SUB), :]

    DYNAMICS, TRACERS = (0, 1, 2), (3, 4)

    def run(outer, number, fields):
        section(outer, number, fields, results_of(outer, number))

    inner = (OWN, SUB)
    outer_rows = (OWN - SUB, 3 * SUB)
    sends = []
    high_sends, low_sends, odd_sends, even_sends = [], [], [], []

    previous = None
    for outer in range(OUTER):
        msg = all_messages(outer)
        if outer == 0:
            for copy in loads_mass:
                copy.wait()
            sum_layers(outer)
            pl.semaphore_wait(barrier, 6)
            start(msg["total"])
            start(msg["mass"])
            for copy in loads_planes:
                copy.wait()

            def count_up(tile):
                rows = pl.ds(OWN + SUB * tile, SUB)
                planes[2, :, rows, :] = active_raw[:, rows, :].astype(jnp.float32)

            tiles(2, count_up)
            start(msg["plane"])
            sends += msg["plane"]
            for copy in loads_wind:
                copy.wait()
            start(msg["wind"])
        else:
            sum_layers(outer)
            start(msg["total"])
            start(msg["mass"])
            start(msg["wind"])
            arrive(previous["trace"])
            run(outer - 1, 0, TRACERS)
        sends += msg["total"] + msg["mass"] + msg["wind"]

        arrive(msg["total"])
        add_planes(outer, pair, total, total_pair)

        @pl.when(is_high)
        def _():
            start(msg["pair"])
            start(msg["pair_edge"])

        @pl.when(is_odd)
        def _():
            start(msg["total_edge"])

        high_sends += msg["pair"] + msg["pair_edge"]
        odd_sends += msg["total_edge"]

        if outer == 0:
            coefficients(inner)
            for copy in loads_trace:
                copy.wait()
        else:
            run(outer - 1, 1, TRACERS)
            run(outer - 1, 2, TRACERS)

        @pl.when(is_low)
        def _():
            arrive(msg["pair"])

        weigh(outer, inner, True)
        start(msg["exner"])
        start(msg["trace"])
        sends += msg["exner"] + msg["trace"]
        arrive(msg["exner"])
        add_planes(outer, low_pair, exner, exner_pair)

        @pl.when(is_low)
        def _():
            start(msg["below"])
            start(msg["below_edge"])

        @pl.when(is_even)
        def _():
            start(msg["exner_edge"])

        low_sends += msg["below"] + msg["below_edge"]
        even_sends += msg["exner_edge"]

        if outer == 0:
            arrive(msg["plane"])
            coefficients(outer_rows)
        arrive(msg["mass"])

        @pl.when(is_odd)
        def _():
            arrive(msg["total_edge"])

        @pl.when(is_low)
        def _():
            arrive(msg["pair_edge"])

        weigh(outer, outer_rows, False)

        @pl.when(is_even)
        def _():
            arrive(msg["exner_edge"])

        @pl.when(is_high)
        def _():
            arrive(msg["below"])
            arrive(msg["below_edge"])

        montgomery(outer)
        arrive(msg["wind"])
        for number in range(3):
            run(outer, number, DYNAMICS)
        previous = msg

    arrive(previous["trace"])
    for number in range(3):
        run(OUTER - 1, number, TRACERS)

    sent(sends)
    for condition, copies in (
        (is_high, high_sends),
        (is_low, low_sends),
        (is_odd, odd_sends),
        (is_even, even_sends),
    ):

        @pl.when(condition)
        def _(copies=copies):
            sent(copies)


def store_kernel(*refs):
    count = (len(refs) - 1) // 2
    sem = refs[-1]
    copies = [
        pltpu.make_async_copy(
            refs[field].at[:, :, pl.ds(SUB * half, SUB), :], refs[count + field].at[:, half], sem.at[field, half]
        )
        for field in range(count)
        for half in range(2)
    ]
    for copy in copies:
        copy.start()
    for copy in copies:
        copy.wait()


def local(row_devices, levels, *arguments):
    fields, theta, maps = arguments[:5], arguments[5], arguments[6:]
    layers, rows, columns = fields[0].shape
    blocks = columns // LANES

    def cut(values):
        lead = values.shape[:-2]
        values = values.reshape(lead + (rows // SUB, SUB, blocks, LANES))
        return pltpu.with_memory_space_constraint(jnp.swapaxes(values, -3, -2), pltpu.HBM)

    def joined(values):
        return jnp.swapaxes(values, -3, -2).reshape(layers, rows, columns)

    anywhere = pl.BlockSpec(memory_space=pltpu.HBM)
    in_vmem = pl.BlockSpec(memory_space=VMEM)
    part = jax.ShapeDtypeStruct((layers, blocks, rows, LANES), jnp.float32)
    plane = VMEM((OUTER, blocks, DEPTH, LANES), jnp.float32)
    volume = VMEM((layers, blocks, DEPTH, LANES), jnp.float32)
    results = pl.pallas_call(
        functools.partial(steps_kernel, levels, columns, row_devices),
        name="layer_steps",
        out_shape=[part] * 5,
        in_specs=[anywhere] * 5 + [pl.BlockSpec(memory_space=pltpu.SMEM)] + [anywhere] * 3,
        out_specs=[in_vmem] * 5,
        scratch_shapes=[
            VMEM((OUTER, 5, layers, blocks, DEPTH, LANES), jnp.float32),
            VMEM((5, layers, blocks, DEPTH, LANES), jnp.float32),
            VMEM((5, layers, blocks, DEPTH, LANES), jnp.float32),
            VMEM((3, blocks, DEPTH, LANES), jnp.float32),
            VMEM((blocks, DEPTH, LANES), jnp.int32),
        ]
        + [plane] * 8
        + [volume] * 7
        + [
            VMEM((blocks, DEPTH, LANES), jnp.float32),
            pltpu.SemaphoreType.DMA((8, 2)),
            pltpu.SemaphoreType.DMA((OUTER, MESSAGES)),
            pltpu.SemaphoreType.DMA((OUTER, MESSAGES)),
        ],
        compiler_params=pltpu.CompilerParams(
            collective_id=0, has_side_effects=True, vmem_limit_bytes=48 * 2**20
        ),
    )(*[cut(values) for values in fields], pltpu.with_memory_space_constraint(theta, pltpu.HBM), *[cut(values) for values in maps])

    stored = pl.pallas_call(
        store_kernel,
        name="store_layers",
        out_shape=[jax.ShapeDtypeStruct((layers, rows // SUB, blocks, SUB, LANES), jnp.float32)] * 5,
        in_specs=[in_vmem] * 5,
        out_specs=[anywhere] * 5,
        scratch_shapes=[pltpu.SemaphoreType.DMA((5, 2))],
        compiler_params=pltpu.CompilerParams(vmem_limit_bytes=2**20),
    )(*results)
    return tuple(joined(values) for values in stored)


def solution(mesh):
    layered = P("lev", "row", None)
    flat = P("row", None)
    row_devices, lev_devices = mesh.shape["row"], mesh.shape["lev"]

    def whole(*arguments):
        levels = arguments[0].shape[0]
        return jax.shard_map(
            functools.partial(local, row_devices, levels),
            mesh=mesh,
            in_specs=(layered,) * 5 + (P(),) + (flat,) * 3,
            out_specs=(layered,) * 5,
            check_vma=False,
        )(*arguments)

    return whole
```

```python
import functools

import jax
import jax.numpy as jnp
from jax import lax
from jax.experimental import pallas as pl
from jax.experimental.pallas import tpu as pltpu
from jax.sharding import PartitionSpec as P

OUTER = 2
SECTIONS = (1.0 / 3.0, 0.5, 1.0)

time_step = 0.05
top_pressure = 0.1
exner_power = 2.0 / 7.0

MESH = pl.DeviceIdType.MESH
VMEM = pltpu.VMEM

PERIOD = 64
HALO = 3
OWN = 12
DEPTH = 40
LANES = 128
SUB = 8

TOTAL, PAIR, PAIR_UP, PAIR_DN, TOTAL_UP, TOTAL_DN = range(6)
EXNER, BELOW, BELOW_UP, BELOW_DN, EXNER_UP, EXNER_DN = range(6, 12)
MASS_UP, MASS_DN, WIND_UP, WIND_DN, ONE_UP, ONE_DN, TWO_UP, TWO_DN, METRIC_UP, METRIC_DN, GROUND_UP, GROUND_DN = range(12, 24)
MESSAGES = 24


def column_gap(a, edge=False):
    lane = lax.broadcasted_iota(jnp.int32, (1,) + a.shape[1:], 2)
    low, high = (a[:1], a[-1:]) if edge else (jnp.zeros_like(a[:1]), jnp.zeros_like(a[:1]))
    east = pltpu.roll(a, LANES - 1, 2)
    west = pltpu.roll(a, 1, 2)
    east = jnp.where(lane == LANES - 1, jnp.concatenate([east[1:], high], 0), east)
    west = jnp.where(lane == 0, jnp.concatenate([low, west[:-1]], 0), west)
    return east - west


def steps_kernel(
    levels,
    columns,
    row_devices,
    period,
    east_in,
    north_in,
    mass_in,
    one_in,
    two_in,
    theta,
    geopot_in,
    metric_in,
    active_in,
    east_out,
    north_out,
    mass_out,
    one_out,
    two_out,
    state,
    first,
    second,
    planes,
    active_raw,
    total,
    total_pair,
    pair,
    above,
    exner,
    exner_pair,
    low_pair,
    below,
    weight,
    potential,
    slope_x,
    slope_y,
    half_metric,
    half_square,
    spin,
    inverse,
    load_sem,
    send_sem,
    recv_sem,
):
    layers, blocks = state.shape[2], state.shape[3]
    lev, row = lax.axis_index("lev"), lax.axis_index("row")
    up_row = lax.rem(row + 1, row_devices)
    dn_row = lax.rem(row + row_devices - 1, row_devices)
    odd = lax.rem(lev, 2)
    core = (lev + 1 - 2 * odd, row)
    far_lev = lax.rem(lev + 2, 4)
    far, far_up, far_dn = (far_lev, row), (far_lev, up_row), (far_lev, dn_row)
    up, dn = (lev, up_row), (lev, dn_row)
    is_odd, is_even = odd == 1, odd == 0
    is_high, is_low = lev < 2, lev >= 2
    own = pl.ds(OWN, 2 * SUB)
    first_layer = lev * layers

    def load(slot, source, target):
        return [
            pltpu.make_async_copy(
                source(half), target(pl.ds(OWN + half * SUB, SUB)), load_sem.at[slot, half]
            )
            for half in range(2)
        ]

    def load_field(slot, ref, field):
        return load(slot, lambda half: ref.at[:, half], lambda rows: state.at[0, field, :, :, rows, :])

    loads_mass = load_field(0, mass_in, 2)
    loads_planes = (
        load(1, lambda half: metric_in.at[half], lambda rows: planes.at[0, :, rows, :])
        + load(2, lambda half: geopot_in.at[half], lambda rows: planes.at[1, :, rows, :])
        + load(3, lambda half: active_in.at[half], lambda rows: active_raw.at[:, rows, :])
    )
    loads_wind = load_field(4, east_in, 0) + load_field(5, north_in, 1)
    loads_trace = load_field(6, one_in, 3) + load_field(7, two_in, 4)
    for copy in loads_mass + loads_planes + loads_wind + loads_trace:
        copy.start()

    early = lax.rem(row, period) == 0
    late = jnp.logical_not(early)
    up_early, dn_early = lax.rem(up_row, period) == 0, lax.rem(dn_row, period) == 0
    barrier = pltpu.get_barrier_semaphore()

    def greet(*devices):
        for device in devices:
            pl.semaphore_signal(barrier, inc=1, device_id=device, device_id_type=MESH)

    greet(core, far)

    @pl.when(late & jnp.logical_not(up_early))
    def _():
        greet(up, far_up)

    @pl.when(late & jnp.logical_not(dn_early))
    def _():
        greet(dn, far_dn)

    def meet():
        @pl.when(early)
        def _():
            pl.semaphore_wait(barrier, 2)
            greet(up, far_up, dn, far_dn)

        @pl.when(late)
        def _():
            pl.semaphore_wait(barrier, 6)

        @pl.when(late & up_early)
        def _():
            greet(up, far_up)

        @pl.when(late & dn_early)
        def _():
            greet(dn, far_dn)

    def message(outer, kind, source, target, device):
        return pltpu.make_async_remote_copy(
            src_ref=source,
            dst_ref=target,
            send_sem=send_sem.at[outer, kind],
            recv_sem=recv_sem.at[outer, kind],
            device_id=device,
            device_id_type=MESH,
        )

    edge_up = (pl.ds(OWN + 2 * SUB - HALO, HALO), pl.ds(OWN - HALO, HALO))
    edge_dn = (pl.ds(OWN, HALO), pl.ds(OWN + 2 * SUB, HALO))

    def edges(outer, kinds, ref, ref_to, to_up, to_dn):
        return [
            message(outer, kind, ref(rows[0]), ref_to(rows[1]), device)
            for kind, rows, device in zip(kinds, (edge_up, edge_dn), (to_up, to_dn))
        ]

    def plane_rows(ref, outer):
        return lambda rows: ref.at[outer, :, rows, :]

    def field_rows(outer, field, count):
        return lambda rows: state.at[outer, pl.ds(field, count), :, :, rows, :]

    def all_messages(outer):
        same = lambda kinds, ref: edges(outer, kinds, ref, ref, up, dn)
        msg = {}
        msg["total"] = [message(outer, TOTAL, total.at[outer, :, own, :], total_pair.at[outer, :, own, :], core)]
        msg["pair"] = [
            message(outer, PAIR, pair.at[outer, :, own, :], above.at[outer, :, own, :], far)
        ]
        msg["pair_edge"] = edges(
            outer, (PAIR_UP, PAIR_DN), plane_rows(pair, outer), plane_rows(above, outer), far_up, far_dn
        )
        msg["total_edge"] = same((TOTAL_UP, TOTAL_DN), plane_rows(total_pair, outer))
        msg["exner"] = [message(outer, EXNER, exner.at[outer, :, own, :], exner_pair.at[outer, :, own, :], core)]
        msg["below"] = [
            message(outer, BELOW, low_pair.at[outer, :, own, :], below.at[outer, :, own, :], far)
        ]
        msg["below_edge"] = edges(
            outer, (BELOW_UP, BELOW_DN), plane_rows(low_pair, outer), plane_rows(below, outer), far_up, far_dn
        )
        msg["exner_edge"] = same((EXNER_UP, EXNER_DN), plane_rows(exner_pair, outer))
        for name, kinds, ref in (
            ("mass", (MASS_UP, MASS_DN), field_rows(outer, 2, 1)),
            ("wind", (WIND_UP, WIND_DN), field_rows(outer, 0, 2)),
            ("one", (ONE_UP, ONE_DN), field_rows(outer, 3, 1)),
            ("two", (TWO_UP, TWO_DN), field_rows(outer, 4, 1)),
            ("metric", (METRIC_UP, METRIC_DN), lambda rows: planes.at[pl.ds(0, 1), :, rows, :]),
            ("ground", (GROUND_UP, GROUND_DN), lambda rows: planes.at[pl.ds(1, 2), :, rows, :]),
        ):
            if name not in ("metric", "ground") or outer == 0:
                msg[name] = same(kinds, ref)
                msg[name + "_up"], msg[name + "_dn"] = msg[name][:1], msg[name][1:]
        return msg

    def start(copies):
        for copy in copies:
            copy.start()

    def arrive(copies):
        for copy in copies:
            copy.wait_recv()

    def sent(copies):
        for copy in copies:
            copy.wait_send()

    def tiles(count, body, unroll=1):
        def one(index, carry):
            body(index)
            return carry

        lax.fori_loop(0, count, one, 0, unroll=unroll)

    def sum_layers(outer):
        def body(tile):
            rows = pl.ds(OWN + SUB * tile, SUB)
            acc = jnp.abs(state[outer, 2, 0, :, rows, :])
            for layer in range(1, layers):
                acc = acc + jnp.abs(state[outer, 2, layer, :, rows, :])
            total[outer, :, rows, :] = acc

        tiles(2, body, 2)

    def add_planes(outer, out, one, other, ground=False):
        def body(tile):
            rows = pl.ds(OWN + SUB * tile, SUB)
            both = one[outer, :, rows, :] + other[outer, :, rows, :]
            out[outer, :, rows, :] = both + planes[1, :, rows, :] if ground else both

        tiles(2, body, 2)

    def weigh(outer, starts, keep_sum):
        base, stride = starts

        def body(tile):
            rows = pl.ds(base + stride * tile, SUB)
            running = jnp.where(is_odd, total_pair[outer, :, rows, :], 0.0) + jnp.where(
                is_low, above[outer, :, rows, :], 0.0
            )
            weighted = []
            for layer in range(layers):
                running = running + jnp.abs(state[outer, 2, layer, :, rows, :])
                pressure = top_pressure + running * (1.0 / levels)
                weighted.append(theta[first_layer + layer] * jnp.exp(exner_power * jnp.log(pressure)))
            acc = weighted[-1]
            weight[layers - 1, :, rows, :] = acc
            for layer in range(layers - 2, -1, -1):
                acc = acc + weighted[layer]
                weight[layer, :, rows, :] = acc
            if keep_sum:
                exner[outer, :, rows, :] = acc

        tiles(2, body)

    def coefficients(starts):
        base, stride = starts
        shape = (blocks, SUB, LANES)
        column = LANES * lax.broadcasted_iota(jnp.int32, shape, 0) + lax.broadcasted_iota(jnp.int32, shape, 2)
        coriolis = 0.5 + column.astype(jnp.float32) / columns

        def body(tile):
            rows = pl.ds(base + stride * tile, SUB)
            metric = planes[0, :, rows, :]
            count = planes[2, :, rows, :]
            inverse[:, rows, :] = 1.0 / metric
            half = 0.5 * metric
            square = half * metric
            for layer in range(layers):
                active = jnp.logical_or(count > (first_layer + layer).astype(jnp.float32), is_high)
                half_metric[layer, :, rows, :] = jnp.where(active, half, 0.0)
                half_square[layer, :, rows, :] = jnp.where(active, square, 0.0)
                spin[layer, :, rows, :] = jnp.where(active, coriolis, 0.0)

        tiles(2, body)

    def montgomery(outer):
        def body(tile):
            rows = pl.ds(OWN - 4 + SUB * tile, SUB)
            rest = jnp.where(is_even, exner_pair[outer, :, rows, :], 0.0) + jnp.where(
                is_high, below[outer, :, rows, :], planes[1, :, rows, :]
            )
            for layer in range(layers):
                potential[layer, :, rows, :] = rest + weight[layer, :, rows, :]

        tiles(3, body, 3)

        def slopes(index):
            layer, tile = index // 3, lax.rem(index, 3)
            base = OWN - 4 + SUB * tile
            rows = pl.ds(base, SUB)
            half = half_metric[layer, :, rows, :]
            along = half * (
                potential[layer, :, pl.ds(base + 1, SUB), :] - potential[layer, :, pl.ds(base - 1, SUB), :]
            )
            across = half * column_gap(potential[layer, :, rows, :], edge=True)
            slope_x[layer, :, rows, :] = along
            slope_y[layer, :, rows, :] = across
            first[0, layer, :, rows, :] = first[0, layer, :, rows, :] - (time_step * SECTIONS[0]) * along
            first[1, layer, :, rows, :] = first[1, layer, :, rows, :] - (time_step * SECTIONS[0]) * across

        tiles(3 * layers, slopes, 4)

    def section(outer, number, fields, results):
        count = 2 if number == 2 else 3
        begin = OWN if number == 2 else OWN - 4
        factor = time_step * SECTIONS[number]
        source = (state.at[outer], first, second)[number]

        def body(index):
            layer, tile = index // count, lax.rem(index, count)
            base = begin + SUB * tile

            def get(ref, field, shift=0):
                return ref[field, layer, :, pl.ds(base + shift, SUB), :]

            def plane(ref):
                return ref[layer, :, pl.ds(base, SUB), :]

            start_of = state.at[outer]
            half = plane(half_metric) * factor
            east, north = get(source, 0), get(source, 1)
            flow_x, flow_y = half * east, half * north

            def carried(field):
                middle = get(source, field)
                return flow_x * (get(source, field, 1) - get(source, field, -1)) + flow_y * column_gap(middle)

            if 0 in fields:
                turn = plane(spin) * factor
                push_x, push_y = turn * north, turn * east
                if number > 0:
                    push_x = push_x - plane(slope_x) * factor
                    push_y = push_y + plane(slope_y) * factor
                results(0, layer, tile)[...] = get(start_of, 0) + push_x - carried(0)
                results(1, layer, tile)[...] = get(start_of, 1) - push_y - carried(1)

                def flux(shift):
                    return get(source, 2, shift) * get(source, 0, shift) * inverse[:, pl.ds(base + shift, SUB), :]

                across = get(source, 2) * north * plane_of(inverse, base)
                results(2, layer, tile)[...] = get(start_of, 2) - factor * plane(half_square) * (
                    (flux(1) - flux(-1)) + column_gap(across)
                )
            for field in fields:
                if field > 2:
                    results(field, layer, tile)[...] = get(start_of, field) - carried(field)

        tiles(count * layers, body, 4)

    def plane_of(ref, base):
        return ref[:, pl.ds(base, SUB), :]

    outputs = (east_out, north_out, mass_out, one_out, two_out)

    def results_of(outer, number):
        if number < 2:
            ref = (first, second)[number]
            return lambda field, layer, tile: ref.at[field, layer, :, pl.ds(OWN - 4 + SUB * tile, SUB), :]
        if outer + 1 < OUTER:
            return lambda field, layer, tile: state.at[outer + 1, field, layer, :, pl.ds(OWN + SUB * tile, SUB), :]
        return lambda field, layer, tile: outputs[field].at[layer, :, pl.ds(SUB * tile, SUB), :]

    DYNAMICS, TRACERS = (0, 1, 2), (3, 4)

    def run(outer, number, fields):
        section(outer, number, fields, results_of(outer, number))

    inner = (OWN, SUB)
    outer_rows = (OWN - SUB, 3 * SUB)
    sends = []
    high_sends, low_sends, odd_sends, even_sends = [], [], [], []

    previous = None
    held_back = []
    for outer in range(OUTER):
        msg = all_messages(outer)

        def to_rows(copies, condition=None, first_step=outer == 0):
            allowed = condition
            if first_step:
                held_back.append((condition, copies))
                allowed = late if condition is None else late & condition
            if allowed is None:
                start(copies)
            else:
                pl.when(allowed)(functools.partial(start, copies))

        if outer == 0:
            for copy in loads_mass:
                copy.wait()
            sum_layers(outer)
            meet()
            start(msg["total"])
            to_rows(msg["mass"])
            for copy in loads_planes:
                copy.wait()

            def count_up(tile):
                rows = pl.ds(OWN + SUB * tile, SUB)
                planes[2, :, rows, :] = active_raw[:, rows, :].astype(jnp.float32)

            tiles(2, count_up)
            to_rows(msg["metric_dn"])
            to_rows(msg["ground_dn"], is_low)
            sends += msg["metric"]
            low_sends += msg["ground"]
            for copy in loads_wind:
                copy.wait()
        else:
            sum_layers(outer)
            start(msg["total"])
            to_rows(msg["mass"])
            arrive(previous["one"] + previous["two"])
            run(outer - 1, 0, TRACERS)
        sends += msg["total"] + msg["mass"] + msg["wind"] + msg["exner"] + msg["one"] + msg["two"]

        arrive(msg["total"])
        add_planes(outer, pair, total, total_pair)

        @pl.when(is_high)
        def _():
            start(msg["pair"])

        to_rows(msg["pair_edge"], is_high)
        to_rows(msg["total_edge"], is_odd)

        high_sends += msg["pair_edge"]
        odd_sends += msg["total_edge"]
        to_rows(msg["wind_dn"])

        if outer == 0:
            coefficients(inner)
            for copy in loads_trace:
                copy.wait()
        else:
            run(outer - 1, 1, TRACERS)

        @pl.when(is_high)
        def _():
            sent(msg["pair"])

        @pl.when(is_low)
        def _():
            arrive(msg["pair"])

        if outer == 0:
            to_rows(msg["metric_up"])
            to_rows(msg["ground_up"], is_low)
        to_rows(msg["wind_up"])
        weigh(outer, inner, True)
        start(msg["exner"])
        if outer > 0:
            run(outer - 1, 2, TRACERS)
        arrive(msg["exner"])
        add_planes(outer, low_pair, exner, exner_pair, ground=True)

        @pl.when(is_low)
        def _():
            start(msg["below"])

        to_rows(msg["below_edge"], is_low)
        to_rows(msg["exner_edge"], is_even)

        low_sends += msg["below_edge"]
        even_sends += msg["exner_edge"]
        to_rows(msg["one_up"] + msg["two_up"])

        if outer == 0:

            @pl.when(early)
            def _():
                pl.semaphore_wait(barrier, 4)
                for condition, copies in held_back:
                    if condition is None:
                        start(copies)
                    else:
                        pl.when(condition)(functools.partial(start, copies))

            arrive(msg["metric"])

            @pl.when(is_low)
            def _():
                arrive(msg["ground"])

            coefficients(outer_rows)
        arrive(msg["mass"])

        @pl.when(is_odd)
        def _():
            arrive(msg["total_edge"])

        @pl.when(is_low)
        def _():
            arrive(msg["pair_edge"])

        weigh(outer, outer_rows, False)

        @pl.when(is_low)
        def _():
            sent(msg["below"])

        @pl.when(is_high)
        def _():
            arrive(msg["below"])

        start(msg["one_dn"] + msg["two_dn"])
        arrive(msg["wind"])
        run(outer, 0, DYNAMICS)

        @pl.when(is_even)
        def _():
            arrive(msg["exner_edge"])

        @pl.when(is_high)
        def _():
            arrive(msg["below_edge"])

        montgomery(outer)
        for number in (1, 2):
            run(outer, number, DYNAMICS)
        previous = msg

    arrive(previous["one"] + previous["two"])
    for number in range(3):
        run(OUTER - 1, number, TRACERS)

    sent(sends)
    for condition, copies in (
        (is_high, high_sends),
        (is_low, low_sends),
        (is_odd, odd_sends),
        (is_even, even_sends),
    ):

        @pl.when(condition)
        def _(copies=copies):
            sent(copies)


def store_kernel(*refs):
    count = (len(refs) - 1) // 2
    sem = refs[-1]
    copies = [
        pltpu.make_async_copy(
            refs[field].at[:, :, pl.ds(SUB * half, SUB), :], refs[count + field].at[:, half], sem.at[field, half]
        )
        for field in range(count)
        for half in range(2)
    ]
    for copy in copies:
        copy.start()
    for copy in copies:
        copy.wait()


def local(row_devices, levels, *arguments):
    fields, theta, maps = arguments[:5], arguments[5], arguments[6:]
    layers, rows, columns = fields[0].shape
    blocks = columns // LANES

    def cut(values):
        lead = values.shape[:-2]
        values = values.reshape(lead + (rows // SUB, SUB, blocks, LANES))
        return pltpu.with_memory_space_constraint(jnp.swapaxes(values, -3, -2), pltpu.HBM)

    def joined(values):
        return jnp.swapaxes(values, -3, -2).reshape(layers, rows, columns)

    anywhere = pl.BlockSpec(memory_space=pltpu.HBM)
    in_vmem = pl.BlockSpec(memory_space=VMEM)
    part = jax.ShapeDtypeStruct((layers, blocks, rows, LANES), jnp.float32)
    plane = VMEM((OUTER, blocks, DEPTH, LANES), jnp.float32)
    volume = VMEM((layers, blocks, DEPTH, LANES), jnp.float32)
    results = pl.pallas_call(
        functools.partial(steps_kernel, levels, columns, row_devices, PERIOD),
        name="layer_steps",
        out_shape=[part] * 5,
        in_specs=[anywhere] * 5 + [pl.BlockSpec(memory_space=pltpu.SMEM)] + [anywhere] * 3,
        out_specs=[in_vmem] * 5,
        scratch_shapes=[
            VMEM((OUTER, 5, layers, blocks, DEPTH, LANES), jnp.float32),
            VMEM((5, layers, blocks, DEPTH, LANES), jnp.float32),
            VMEM((5, layers, blocks, DEPTH, LANES), jnp.float32),
            VMEM((3, blocks, DEPTH, LANES), jnp.float32),
            VMEM((blocks, DEPTH, LANES), jnp.int32),
        ]
        + [plane] * 8
        + [volume] * 7
        + [
            VMEM((blocks, DEPTH, LANES), jnp.float32),
            pltpu.SemaphoreType.DMA((8, 2)),
            pltpu.SemaphoreType.DMA((OUTER, MESSAGES)),
            pltpu.SemaphoreType.DMA((OUTER, MESSAGES)),
        ],
        compiler_params=pltpu.CompilerParams(
            collective_id=0, has_side_effects=True, vmem_limit_bytes=48 * 2**20
        ),
    )(*[cut(values) for values in fields], pltpu.with_memory_space_constraint(theta, pltpu.HBM), *[cut(values) for values in maps])

    stored = pl.pallas_call(
        store_kernel,
        name="store_layers",
        out_shape=[jax.ShapeDtypeStruct((layers, rows // SUB, blocks, SUB, LANES), jnp.float32)] * 5,
        in_specs=[in_vmem] * 5,
        out_specs=[anywhere] * 5,
        scratch_shapes=[pltpu.SemaphoreType.DMA((5, 2))],
        compiler_params=pltpu.CompilerParams(vmem_limit_bytes=2**20),
    )(*results)
    return tuple(joined(values) for values in stored)


def solution(mesh):
    layered = P("lev", "row", None)
    flat = P("row", None)
    row_devices, lev_devices = mesh.shape["row"], mesh.shape["lev"]

    def whole(*arguments):
        levels = arguments[0].shape[0]
        return jax.shard_map(
            functools.partial(local, row_devices, levels),
            mesh=mesh,
            in_specs=(layered,) * 5 + (P(),) + (flat,) * 3,
            out_specs=(layered,) * 5,
            check_vma=False,
        )(*arguments)

    return whole
```

```python
import functools

import jax
import jax.numpy as jnp
from jax import lax
from jax.experimental import pallas as pl
from jax.experimental.pallas import tpu as pltpu
from jax.sharding import PartitionSpec as P

OUTER = 2
SECTIONS = (1.0 / 3.0, 0.5, 1.0)

time_step = 0.05
top_pressure = 0.1
exner_power = 2.0 / 7.0

MESH = pl.DeviceIdType.MESH
VMEM = pltpu.VMEM

PERIOD = 64
HALO = 3
OWN = 12
DEPTH = 40
LANES = 128
SUB = 8

SHARE, SHARE_LOW, SHARE_HIGH, TOTAL, TOTAL_UP, TOTAL_DN = range(6)
EXNER, EXNER_UP, EXNER_DN, GIVE, GIVE_LOW, GIVE_HIGH, BELOW, CROSS_UP, CROSS_DN = range(6, 15)
MASS_UP, MASS_DN, WIND_UP, WIND_DN, ONE_UP, ONE_DN, TWO_UP, TWO_DN = range(15, 23)
METRIC_UP, METRIC_DN, GROUND_UP, GROUND_DN = range(23, 27)
MESSAGES = 27


def column_gap(a, edge=False):
    lane = lax.broadcasted_iota(jnp.int32, (1,) + a.shape[1:], 2)
    low, high = (a[:1], a[-1:]) if edge else (jnp.zeros_like(a[:1]), jnp.zeros_like(a[:1]))
    east = pltpu.roll(a, LANES - 1, 2)
    west = pltpu.roll(a, 1, 2)
    east = jnp.where(lane == LANES - 1, jnp.concatenate([east[1:], high], 0), east)
    west = jnp.where(lane == 0, jnp.concatenate([low, west[:-1]], 0), west)
    return east - west


def steps_kernel(
    levels,
    columns,
    row_devices,
    period,
    east_in,
    north_in,
    mass_in,
    one_in,
    two_in,
    theta,
    geopot_in,
    metric_in,
    active_in,
    east_out,
    north_out,
    mass_out,
    one_out,
    two_out,
    state,
    first,
    second,
    planes,
    active_raw,
    total,
    above,
    exner,
    below,
    shared,
    given,
    weight,
    potential,
    slope_x,
    slope_y,
    half_metric,
    half_square,
    spin,
    inverse,
    load_sem,
    send_sem,
    recv_sem,
):
    layers, blocks = state.shape[2], state.shape[3]
    lev, row = lax.axis_index("lev"), lax.axis_index("row")
    up_row = lax.rem(row + 1, row_devices)
    dn_row = lax.rem(row + row_devices - 1, row_devices)
    odd = lax.rem(lev, 2)
    core = (lev + 1 - 2 * odd, row)
    far_lev = lax.rem(lev + 2, 4)
    far, far_up, far_dn = (far_lev, row), (far_lev, up_row), (far_lev, dn_row)
    up, dn = (lev, up_row), (lev, dn_row)
    cross_lev = far_lev + 1 - 2 * odd
    cross_up, cross_dn = (cross_lev, up_row), (cross_lev, dn_row)
    is_even = odd == 0
    half_blocks = blocks // 2
    mine = pl.ds(odd * half_blocks, half_blocks)
    theirs = pl.ds((1 - odd) * half_blocks, half_blocks)
    is_high, is_low = lev < 2, lev >= 2
    own = pl.ds(OWN, 2 * SUB)
    first_layer = lev * layers

    def load(slot, source, target):
        return [
            pltpu.make_async_copy(
                source(half), target(pl.ds(OWN + half * SUB, SUB)), load_sem.at[slot, half]
            )
            for half in range(2)
        ]

    def load_field(slot, ref, field):
        return load(slot, lambda half: ref.at[:, half], lambda rows: state.at[0, field, :, :, rows, :])

    loads_mass = load_field(0, mass_in, 2)
    loads_planes = (
        load(1, lambda half: metric_in.at[half], lambda rows: planes.at[0, :, rows, :])
        + load(2, lambda half: geopot_in.at[half], lambda rows: planes.at[1, :, rows, :])
        + load(3, lambda half: active_in.at[half], lambda rows: active_raw.at[:, rows, :])
    )
    loads_wind = load_field(4, east_in, 0) + load_field(5, north_in, 1)
    loads_trace = load_field(6, one_in, 3) + load_field(7, two_in, 4)
    for copy in loads_mass + loads_planes + loads_wind + loads_trace:
        copy.start()

    early = lax.rem(row, period) == 0
    late = jnp.logical_not(early)
    up_early, dn_early = lax.rem(up_row, period) == 0, lax.rem(dn_row, period) == 0
    barrier = pltpu.get_barrier_semaphore()

    def greet(*devices):
        for device in devices:
            pl.semaphore_signal(barrier, inc=1, device_id=device, device_id_type=MESH)

    greet(core, far)

    @pl.when(late & jnp.logical_not(up_early))
    def _():
        greet(up, far_up, cross_up)

    @pl.when(late & jnp.logical_not(dn_early))
    def _():
        greet(dn, far_dn, cross_dn)

    def meet():
        @pl.when(early)
        def _():
            pl.semaphore_wait(barrier, 2)
            greet(up, far_up, cross_up, dn, far_dn, cross_dn)

        @pl.when(late)
        def _():
            pl.semaphore_wait(barrier, 8)

        @pl.when(late & up_early)
        def _():
            greet(up, far_up, cross_up)

        @pl.when(late & dn_early)
        def _():
            greet(dn, far_dn, cross_dn)

    def message(outer, kind, source, target, device):
        return pltpu.make_async_remote_copy(
            src_ref=source,
            dst_ref=target,
            send_sem=send_sem.at[outer, kind],
            recv_sem=recv_sem.at[outer, kind],
            device_id=device,
            device_id_type=MESH,
        )

    edge_up = (pl.ds(OWN + 2 * SUB - HALO, HALO), pl.ds(OWN - HALO, HALO))
    edge_dn = (pl.ds(OWN, HALO), pl.ds(OWN + 2 * SUB, HALO))

    def edges(outer, kinds, ref, ref_to, to_up, to_dn):
        return [
            message(outer, kind, ref(rows[0]), ref_to(rows[1]), device)
            for kind, rows, device in zip(kinds, (edge_up, edge_dn), (to_up, to_dn))
        ]

    def plane_rows(ref, outer):
        return lambda rows: ref.at[outer, :, rows, :]

    def field_rows(outer, field, count):
        return lambda rows: state.at[outer, pl.ds(field, count), :, :, rows, :]

    def all_messages(outer):
        same = lambda kinds, ref: edges(outer, kinds, ref, ref, up, dn)
        msg = {}
        low_rows, high_rows = edge_up[1], edge_dn[1]

        def to_core(kinds, ref, ref_to):
            return [
                message(outer, kind, ref(rows), ref_to(rows), core)
                for kind, rows in zip(kinds, (own, low_rows, high_rows))
            ]

        half_below = lambda rows: below.at[outer, mine, rows, :]
        for name, copies in (
            (
                "share",
                to_core(
                    (SHARE, SHARE_LOW, SHARE_HIGH),
                    lambda rows: state.at[outer, 2, :, theirs, rows, :],
                    lambda rows: shared.at[outer, :, :, rows, :],
                ),
            ),
            (
                "give",
                to_core(
                    (GIVE, GIVE_LOW, GIVE_HIGH),
                    lambda rows: given.at[outer, :, :, rows, :],
                    lambda rows: weight.at[outer, :, mine, rows, :],
                ),
            ),
        ):
            msg[name], msg[name + "_edge"] = copies[:1], copies[1:]
        msg["total"] = [message(outer, TOTAL, total.at[outer, :, own, :], above.at[outer, :, own, :], far)]
        msg["total_edge"] = edges(
            outer, (TOTAL_UP, TOTAL_DN), plane_rows(total, outer), plane_rows(above, outer), far_up, far_dn
        )
        msg["exner"] = [message(outer, EXNER, exner.at[outer, :, own, :], half_below(own), far)]
        msg["below"] = [message(outer, BELOW, half_below(own), half_below(own), core)]
        msg["exner_edge"] = edges(
            outer, (EXNER_UP, EXNER_DN), plane_rows(exner, outer), half_below, far_up, far_dn
        ) + edges(outer, (CROSS_UP, CROSS_DN), plane_rows(exner, outer), half_below, cross_up, cross_dn)
        for name, kinds, ref in (
            ("mass", (MASS_UP, MASS_DN), field_rows(outer, 2, 1)),
            ("wind", (WIND_UP, WIND_DN), field_rows(outer, 0, 2)),
            ("one", (ONE_UP, ONE_DN), field_rows(outer, 3, 1)),
            ("two", (TWO_UP, TWO_DN), field_rows(outer, 4, 1)),
            ("metric", (METRIC_UP, METRIC_DN), lambda rows: planes.at[pl.ds(0, 1), :, rows, :]),
            ("ground", (GROUND_UP, GROUND_DN), lambda rows: planes.at[pl.ds(1, 2), :, rows, :]),
        ):
            if name not in ("metric", "ground") or outer == 0:
                msg[name] = same(kinds, ref)
                msg[name + "_up"], msg[name + "_dn"] = msg[name][:1], msg[name][1:]
        return msg

    def start(copies):
        for copy in copies:
            copy.start()

    def arrive(copies):
        for copy in copies:
            copy.wait_recv()

    def sent(copies):
        for copy in copies:
            copy.wait_send()

    def tiles(count, body, unroll=1):
        def one(index, carry):
            body(index)
            return carry

        lax.fori_loop(0, count, one, 0, unroll=unroll)

    def sum_layers(outer):
        def body(tile):
            rows = pl.ds(OWN + SUB * tile, SUB)
            acc = jnp.abs(state[outer, 2, 0, mine, rows, :]) + jnp.abs(shared[outer, 0, :, rows, :])
            for layer in range(1, layers):
                acc = acc + (jnp.abs(state[outer, 2, layer, mine, rows, :]) + jnp.abs(shared[outer, layer, :, rows, :]))
            total[outer, :, rows, :] = acc

        tiles(2, body, 2)

    def weigh(outer, starts, keep_sum):
        base, stride = starts
        chip_layer = first_layer - odd * layers

        def body(tile):
            rows = pl.ds(base + stride * tile, SUB)
            running = jnp.where(is_low, above[outer, :, rows, :], 0.0)
            ours = [state[outer, 2, layer, mine, rows, :] for layer in range(layers)]
            others = [shared[outer, layer, :, rows, :] for layer in range(layers)]
            column = [jnp.where(is_even, a, b) for a, b in zip(ours, others)]
            column += [jnp.where(is_even, b, a) for a, b in zip(ours, others)]
            sums = []
            for layer, mass in enumerate(column):
                running = running + jnp.abs(mass)
                pressure = top_pressure + running * (1.0 / levels)
                sums.append(theta[chip_layer + layer] * jnp.exp(exner_power * jnp.log(pressure)))
            for layer in range(2 * layers - 2, -1, -1):
                sums[layer] = sums[layer] + sums[layer + 1]
            for layer in range(layers):
                upper, lower = sums[layer], sums[layer + layers]
                weight[outer, layer, mine, rows, :] = jnp.where(is_even, upper, lower)
                given[outer, layer, :, rows, :] = jnp.where(is_even, lower, upper)
            if keep_sum:
                exner[outer, :, rows, :] = sums[0] + planes[1, mine, rows, :]

        tiles(2, body)

    def coefficients(starts):
        base, stride = starts
        shape = (blocks, SUB, LANES)
        column = LANES * lax.broadcasted_iota(jnp.int32, shape, 0) + lax.broadcasted_iota(jnp.int32, shape, 2)
        coriolis = 0.5 + column.astype(jnp.float32) / columns

        def body(tile):
            rows = pl.ds(base + stride * tile, SUB)
            metric = planes[0, :, rows, :]
            count = planes[2, :, rows, :]
            inverse[:, rows, :] = 1.0 / metric
            half = 0.5 * metric
            square = half * metric
            for layer in range(layers):
                active = jnp.logical_or(count > (first_layer + layer).astype(jnp.float32), is_high)
                half_metric[layer, :, rows, :] = jnp.where(active, half, 0.0)
                half_square[layer, :, rows, :] = jnp.where(active, square, 0.0)
                spin[layer, :, rows, :] = jnp.where(active, coriolis, 0.0)

        tiles(2, body)

    def montgomery(outer, starts):
        base, stride = starts

        def body(tile):
            rows = pl.ds(base + stride * tile, SUB)
            rest = jnp.where(is_high, below[outer, :, rows, :], planes[1, :, rows, :])
            for layer in range(layers):
                potential[layer, :, rows, :] = rest + weight[outer, layer, :, rows, :]

        tiles(2, body, 2)

    def slopes(picked):
        def body(index):
            layer, tile = pick(picked, index)
            base = OWN - 4 + SUB * tile
            rows = pl.ds(base, SUB)
            half = half_metric[layer, :, rows, :]
            along = half * (
                potential[layer, :, pl.ds(base + 1, SUB), :] - potential[layer, :, pl.ds(base - 1, SUB), :]
            )
            across = half * column_gap(potential[layer, :, rows, :], edge=True)
            slope_x[layer, :, rows, :] = along
            slope_y[layer, :, rows, :] = across
            first[0, layer, :, rows, :] = first[0, layer, :, rows, :] - (time_step * SECTIONS[0]) * along
            first[1, layer, :, rows, :] = first[1, layer, :, rows, :] - (time_step * SECTIONS[0]) * across

        tiles(picked[0] * layers, body, 4)

    def pick(picked, index):
        count, begin, stride = picked
        return index // count, begin + stride * lax.rem(index, count)

    def section(outer, number, fields, results, picked=None):
        picked = picked or (2 if number == 2 else 3, 0, 1)
        begin = OWN if number == 2 else OWN - 4
        factor = time_step * SECTIONS[number]
        source = (state.at[outer], first, second)[number]

        def body(index):
            layer, tile = pick(picked, index)
            base = begin + SUB * tile

            def get(ref, field, shift=0):
                return ref[field, layer, :, pl.ds(base + shift, SUB), :]

            def plane(ref):
                return ref[layer, :, pl.ds(base, SUB), :]

            start_of = state.at[outer]
            half = plane(half_metric) * factor
            east, north = get(source, 0), get(source, 1)
            flow_x, flow_y = half * east, half * north

            def carried(field):
                middle = get(source, field)
                return flow_x * (get(source, field, 1) - get(source, field, -1)) + flow_y * column_gap(middle)

            if 0 in fields:
                turn = plane(spin) * factor
                push_x, push_y = turn * north, turn * east
                if number > 0:
                    push_x = push_x - plane(slope_x) * factor
                    push_y = push_y + plane(slope_y) * factor
                results(0, layer, tile)[...] = get(start_of, 0) + push_x - carried(0)
                results(1, layer, tile)[...] = get(start_of, 1) - push_y - carried(1)

                def flux(shift):
                    return get(source, 2, shift) * get(source, 0, shift) * inverse[:, pl.ds(base + shift, SUB), :]

                across = get(source, 2) * north * plane_of(inverse, base)
                results(2, layer, tile)[...] = get(start_of, 2) - factor * plane(half_square) * (
                    (flux(1) - flux(-1)) + column_gap(across)
                )
            for field in fields:
                if field > 2:
                    results(field, layer, tile)[...] = get(start_of, field) - carried(field)

        tiles(picked[0] * layers, body, 4)

    def plane_of(ref, base):
        return ref[:, pl.ds(base, SUB), :]

    outputs = (east_out, north_out, mass_out, one_out, two_out)

    def results_of(outer, number):
        if number < 2:
            ref = (first, second)[number]
            return lambda field, layer, tile: ref.at[field, layer, :, pl.ds(OWN - 4 + SUB * tile, SUB), :]
        if outer + 1 < OUTER:
            return lambda field, layer, tile: state.at[outer + 1, field, layer, :, pl.ds(OWN + SUB * tile, SUB), :]
        return lambda field, layer, tile: outputs[field].at[layer, :, pl.ds(SUB * tile, SUB), :]

    DYNAMICS, TRACERS = (0, 1, 2), (3, 4)

    def run(outer, number, fields, picked=None):
        section(outer, number, fields, results_of(outer, number), picked)

    middle, beside = (1, 1, 0), (2, 0, 2)

    inner = (OWN, SUB)
    outer_rows = (OWN - SUB, 3 * SUB)
    sends, high_sends, low_sends = [], [], []
    previous = None
    held_back = []
    for outer in range(OUTER):
        msg = all_messages(outer)

        def to_rows(copies, condition=None, first_step=outer == 0):
            allowed = condition
            if first_step:
                held_back.append((condition, copies))
                allowed = late if condition is None else late & condition
            if allowed is None:
                start(copies)
            else:
                pl.when(allowed)(functools.partial(start, copies))

        sends += msg["share"] + msg["share_edge"] + msg["give"] + msg["give_edge"]
        sends += msg["mass"] + msg["wind"] + msg["one"] + msg["two"]
        high_sends += msg["total_edge"] + msg["below"]
        low_sends += msg["exner_edge"]

        if outer == 0:
            for copy in loads_mass:
                copy.wait()
            meet()
            start(msg["share"])
            to_rows(msg["mass"])
            for copy in loads_planes:
                copy.wait()

            def count_up(tile):
                rows = pl.ds(OWN + SUB * tile, SUB)
                planes[2, :, rows, :] = active_raw[:, rows, :].astype(jnp.float32)

            tiles(2, count_up)
            to_rows(msg["metric_dn"])
            to_rows(msg["ground_dn"], is_low)
            sends += msg["metric"]
            low_sends += msg["ground"]
            for copy in loads_wind:
                copy.wait()
        else:
            start(msg["share"])
            to_rows(msg["mass"])

        arrive(msg["share"])

        @pl.when(is_high)
        def _():
            sum_layers(outer)
            start(msg["total"])

        to_rows(msg["total_edge"], is_high)
        to_rows(msg["wind_dn"])

        if outer == 0:
            coefficients(inner)
            for copy in loads_trace:
                copy.wait()

        @pl.when(is_low)
        def _():
            arrive(msg["total"])

        weigh(outer, inner, True)
        start(msg["give"])

        @pl.when(is_low)
        def _():
            start(msg["exner"])

        to_rows(msg["exner_edge"], is_low)

        @pl.when(is_high)
        def _():
            sent(msg["total"])

        if outer == 0:
            to_rows(msg["metric_up"])
            to_rows(msg["ground_up"], is_low)
        to_rows(msg["wind_up"])
        if outer > 0:
            arrive(previous["one"] + previous["two"])
            for number in range(3):
                run(outer - 1, number, TRACERS)
        to_rows(msg["one_up"] + msg["two_up"])

        if outer == 0:

            @pl.when(early)
            def _():
                pl.semaphore_wait(barrier, 6)
                for condition, copies in held_back:
                    if condition is None:
                        start(copies)
                    else:
                        pl.when(condition)(functools.partial(start, copies))

            arrive(msg["metric"])

            @pl.when(is_low)
            def _():
                arrive(msg["ground"])

            coefficients(outer_rows)
        arrive(msg["mass"])
        start(msg["share_edge"])

        @pl.when(is_low)
        def _():
            sent(msg["exner"])

        @pl.when(is_high)
        def _():
            arrive(msg["exner"])
            start(msg["below"])

        start(msg["one_dn"] + msg["two_dn"])
        arrive(msg["share_edge"])

        @pl.when(is_low)
        def _():
            arrive(msg["total_edge"])

        weigh(outer, outer_rows, False)
        start(msg["give_edge"])

        run(outer, 0, DYNAMICS, middle)
        arrive(msg["give"])

        @pl.when(is_high)
        def _():
            arrive(msg["below"])

        montgomery(outer, inner)
        slopes(middle)
        arrive(msg["wind"])
        run(outer, 0, DYNAMICS, beside)
        arrive(msg["give_edge"])

        @pl.when(is_high)
        def _():
            arrive(msg["exner_edge"])

        montgomery(outer, outer_rows)
        slopes(beside)
        for number in (1, 2):
            run(outer, number, DYNAMICS)
        previous = msg

    arrive(previous["one"] + previous["two"])
    for number in range(3):
        run(OUTER - 1, number, TRACERS)

    sent(sends)
    for condition, copies in (
        (is_high, high_sends),
        (is_low, low_sends),
    ):

        @pl.when(condition)
        def _(copies=copies):
            sent(copies)


def store_kernel(*refs):
    count = (len(refs) - 1) // 2
    sem = refs[-1]
    copies = [
        pltpu.make_async_copy(
            refs[field].at[:, :, pl.ds(SUB * half, SUB), :], refs[count + field].at[:, half], sem.at[field, half]
        )
        for field in range(count)
        for half in range(2)
    ]
    for copy in copies:
        copy.start()
    for copy in copies:
        copy.wait()


def local(row_devices, levels, *arguments):
    fields, theta, maps = arguments[:5], arguments[5], arguments[6:]
    layers, rows, columns = fields[0].shape
    blocks = columns // LANES

    def cut(values):
        lead = values.shape[:-2]
        values = values.reshape(lead + (rows // SUB, SUB, blocks, LANES))
        return pltpu.with_memory_space_constraint(jnp.swapaxes(values, -3, -2), pltpu.HBM)

    def joined(values):
        return jnp.swapaxes(values, -3, -2).reshape(layers, rows, columns)

    anywhere = pl.BlockSpec(memory_space=pltpu.HBM)
    in_vmem = pl.BlockSpec(memory_space=VMEM)
    part = jax.ShapeDtypeStruct((layers, blocks, rows, LANES), jnp.float32)
    half_plane = VMEM((OUTER, blocks // 2, DEPTH, LANES), jnp.float32)
    volume = VMEM((layers, blocks, DEPTH, LANES), jnp.float32)
    results = pl.pallas_call(
        functools.partial(steps_kernel, levels, columns, row_devices, PERIOD),
        name="layer_steps",
        out_shape=[part] * 5,
        in_specs=[anywhere] * 5 + [pl.BlockSpec(memory_space=pltpu.SMEM)] + [anywhere] * 3,
        out_specs=[in_vmem] * 5,
        scratch_shapes=[
            VMEM((OUTER, 5, layers, blocks, DEPTH, LANES), jnp.float32),
            VMEM((5, layers, blocks, DEPTH, LANES), jnp.float32),
            VMEM((5, layers, blocks, DEPTH, LANES), jnp.float32),
            VMEM((3, blocks, DEPTH, LANES), jnp.float32),
            VMEM((blocks, DEPTH, LANES), jnp.int32),
        ]
        + [half_plane] * 3
        + [VMEM((OUTER, blocks, DEPTH, LANES), jnp.float32)]
        + [VMEM((OUTER, layers, blocks // 2, DEPTH, LANES), jnp.float32)] * 2
        + [VMEM((OUTER, layers, blocks, DEPTH, LANES), jnp.float32)]
        + [volume] * 6
        + [
            VMEM((blocks, DEPTH, LANES), jnp.float32),
            pltpu.SemaphoreType.DMA((8, 2)),
            pltpu.SemaphoreType.DMA((OUTER, MESSAGES)),
            pltpu.SemaphoreType.DMA((OUTER, MESSAGES)),
        ],
        compiler_params=pltpu.CompilerParams(
            collective_id=0, has_side_effects=True, vmem_limit_bytes=48 * 2**20
        ),
    )(*[cut(values) for values in fields], pltpu.with_memory_space_constraint(theta, pltpu.HBM), *[cut(values) for values in maps])

    stored = pl.pallas_call(
        store_kernel,
        name="store_layers",
        out_shape=[jax.ShapeDtypeStruct((layers, rows // SUB, blocks, SUB, LANES), jnp.float32)] * 5,
        in_specs=[in_vmem] * 5,
        out_specs=[anywhere] * 5,
        scratch_shapes=[pltpu.SemaphoreType.DMA((5, 2))],
        compiler_params=pltpu.CompilerParams(vmem_limit_bytes=2**20),
    )(*results)
    return tuple(joined(values) for values in stored)


def solution(mesh):
    layered = P("lev", "row", None)
    flat = P("row", None)
    row_devices, lev_devices = mesh.shape["row"], mesh.shape["lev"]

    def whole(*arguments):
        levels = arguments[0].shape[0]
        return jax.shard_map(
            functools.partial(local, row_devices, levels),
            mesh=mesh,
            in_specs=(layered,) * 5 + (P(),) + (flat,) * 3,
            out_specs=(layered,) * 5,
            check_vma=False,
        )(*arguments)

    return whole
```

```python
import functools

import jax
import jax.numpy as jnp
from jax import lax
from jax.experimental import pallas as pl
from jax.experimental.pallas import tpu as pltpu
from jax.sharding import PartitionSpec as P

OUTER = 2
SECTIONS = (1.0 / 3.0, 0.5, 1.0)

time_step = 0.05
top_pressure = 0.1
exner_power = 2.0 / 7.0

MESH = pl.DeviceIdType.MESH
VMEM = pltpu.VMEM

PERIOD = 64
HALO = 3
OWN = 12
DEPTH = 40
LANES = 128
SUB = 8

SHARE, SHARE_LOW, SHARE_HIGH, TOTAL, TOTAL_UP, TOTAL_DN = range(6)
EXNER, EXNER_UP, EXNER_DN, GIVE, GIVE_LOW, GIVE_HIGH, BELOW, CROSS_UP, CROSS_DN = range(6, 15)
MASS_UP, MASS_DN, WIND_UP, WIND_DN, ONE_UP, ONE_DN, TWO_UP, TWO_DN = range(15, 23)
METRIC_UP, METRIC_DN, GROUND_UP, GROUND_DN = range(23, 27)
MESSAGES = 27


def column_gap(a, edge=False):
    lane = lax.broadcasted_iota(jnp.int32, (1,) + a.shape[1:], 2)
    low, high = (a[:1], a[-1:]) if edge else (jnp.zeros_like(a[:1]), jnp.zeros_like(a[:1]))
    east = pltpu.roll(a, LANES - 1, 2)
    west = pltpu.roll(a, 1, 2)
    east = jnp.where(lane == LANES - 1, jnp.concatenate([east[1:], high], 0), east)
    west = jnp.where(lane == 0, jnp.concatenate([low, west[:-1]], 0), west)
    return east - west


def steps_kernel(
    levels,
    columns,
    row_devices,
    period,
    east_in,
    north_in,
    mass_in,
    one_in,
    two_in,
    theta,
    geopot_in,
    metric_in,
    active_in,
    east_out,
    north_out,
    mass_out,
    one_out,
    two_out,
    state,
    first,
    second,
    planes,
    active_raw,
    total,
    above,
    exner,
    below,
    shared,
    given,
    weight,
    potential,
    slope_x,
    slope_y,
    half_metric,
    half_square,
    spin,
    inverse,
    load_sem,
    send_sem,
    recv_sem,
):
    layers, blocks = state.shape[2], state.shape[3]
    lev, row = lax.axis_index("lev"), lax.axis_index("row")
    up_row = lax.rem(row + 1, row_devices)
    dn_row = lax.rem(row + row_devices - 1, row_devices)
    odd = lax.rem(lev, 2)
    core = (lev + 1 - 2 * odd, row)
    far_lev = lax.rem(lev + 2, 4)
    far, far_up, far_dn = (far_lev, row), (far_lev, up_row), (far_lev, dn_row)
    up, dn = (lev, up_row), (lev, dn_row)
    cross_lev = far_lev + 1 - 2 * odd
    cross_up, cross_dn = (cross_lev, up_row), (cross_lev, dn_row)
    is_even = odd == 0
    half_blocks = blocks // 2
    mine = pl.ds(odd * half_blocks, half_blocks)
    theirs = pl.ds((1 - odd) * half_blocks, half_blocks)
    is_high, is_low = lev < 2, lev >= 2
    own = pl.ds(OWN, 2 * SUB)
    first_layer = lev * layers

    def load(slot, source, target):
        return [
            pltpu.make_async_copy(
                source(half), target(pl.ds(OWN + half * SUB, SUB)), load_sem.at[slot, half]
            )
            for half in range(2)
        ]

    def load_field(slot, ref, field):
        return load(slot, lambda half: ref.at[:, half], lambda rows: state.at[0, field, :, :, rows, :])

    loads_mass = load_field(0, mass_in, 2)
    loads_planes = (
        load(1, lambda half: metric_in.at[half], lambda rows: planes.at[0, :, rows, :])
        + load(2, lambda half: geopot_in.at[half], lambda rows: planes.at[1, :, rows, :])
        + load(3, lambda half: active_in.at[half], lambda rows: active_raw.at[:, rows, :])
    )
    loads_wind = load_field(4, east_in, 0) + load_field(5, north_in, 1)
    loads_trace = load_field(6, one_in, 3) + load_field(7, two_in, 4)
    for copy in loads_mass + loads_planes + loads_wind + loads_trace:
        copy.start()

    early = lax.rem(row, period) == 0
    late = jnp.logical_not(early)
    up_early, dn_early = lax.rem(up_row, period) == 0, lax.rem(dn_row, period) == 0
    barrier = pltpu.get_barrier_semaphore()

    def greet(*devices):
        for device in devices:
            pl.semaphore_signal(barrier, inc=1, device_id=device, device_id_type=MESH)

    greet(core, far)

    @pl.when(late & jnp.logical_not(up_early))
    def _():
        greet(up, far_up, cross_up)

    @pl.when(late & jnp.logical_not(dn_early))
    def _():
        greet(dn, far_dn, cross_dn)

    def meet():
        @pl.when(early)
        def _():
            pl.semaphore_wait(barrier, 2)
            greet(up, far_up, cross_up, dn, far_dn, cross_dn)

        @pl.when(late)
        def _():
            pl.semaphore_wait(barrier, 8)

        @pl.when(late & up_early)
        def _():
            greet(up, far_up, cross_up)

        @pl.when(late & dn_early)
        def _():
            greet(dn, far_dn, cross_dn)

    def message(outer, kind, source, target, device):
        return pltpu.make_async_remote_copy(
            src_ref=source,
            dst_ref=target,
            send_sem=send_sem.at[outer, kind],
            recv_sem=recv_sem.at[outer, kind],
            device_id=device,
            device_id_type=MESH,
        )

    edge_up = (pl.ds(OWN + 2 * SUB - HALO, HALO), pl.ds(OWN - HALO, HALO))
    edge_dn = (pl.ds(OWN, HALO), pl.ds(OWN + 2 * SUB, HALO))

    def edges(outer, kinds, ref, ref_to, to_up, to_dn):
        return [
            message(outer, kind, ref(rows[0]), ref_to(rows[1]), device)
            for kind, rows, device in zip(kinds, (edge_up, edge_dn), (to_up, to_dn))
        ]

    def plane_rows(ref, outer):
        return lambda rows: ref.at[outer, :, rows, :]

    def field_rows(outer, field, count):
        return lambda rows: state.at[outer, pl.ds(field, count), :, :, rows, :]

    def all_messages(outer):
        same = lambda kinds, ref: edges(outer, kinds, ref, ref, up, dn)
        msg = {}
        low_rows, high_rows = edge_up[1], edge_dn[1]

        def to_core(kinds, ref, ref_to):
            return [
                message(outer, kind, ref(rows), ref_to(rows), core)
                for kind, rows in zip(kinds, (own, low_rows, high_rows))
            ]

        half_below = lambda rows: below.at[outer, mine, rows, :]
        for name, copies in (
            (
                "share",
                to_core(
                    (SHARE, SHARE_LOW, SHARE_HIGH),
                    lambda rows: state.at[outer, 2, :, theirs, rows, :],
                    lambda rows: shared.at[outer, :, :, rows, :],
                ),
            ),
            (
                "give",
                to_core(
                    (GIVE, GIVE_LOW, GIVE_HIGH),
                    lambda rows: given.at[outer, :, :, rows, :],
                    lambda rows: weight.at[outer, :, mine, rows, :],
                ),
            ),
        ):
            msg[name], msg[name + "_edge"] = copies[:1], copies[1:]
        msg["total"] = [message(outer, TOTAL, total.at[outer, :, own, :], above.at[outer, :, own, :], far)]
        msg["total_edge"] = edges(
            outer, (TOTAL_UP, TOTAL_DN), plane_rows(total, outer), plane_rows(above, outer), far_up, far_dn
        )
        msg["exner"] = [message(outer, EXNER, exner.at[outer, :, own, :], half_below(own), far)]
        msg["below"] = [message(outer, BELOW, half_below(own), half_below(own), core)]
        msg["exner_edge"] = edges(
            outer, (EXNER_UP, EXNER_DN), plane_rows(exner, outer), half_below, far_up, far_dn
        ) + edges(outer, (CROSS_UP, CROSS_DN), plane_rows(exner, outer), half_below, cross_up, cross_dn)
        for name, kinds, ref in (
            ("mass", (MASS_UP, MASS_DN), field_rows(outer, 2, 1)),
            ("wind", (WIND_UP, WIND_DN), field_rows(outer, 0, 2)),
            ("one", (ONE_UP, ONE_DN), field_rows(outer, 3, 1)),
            ("two", (TWO_UP, TWO_DN), field_rows(outer, 4, 1)),
            ("metric", (METRIC_UP, METRIC_DN), lambda rows: planes.at[pl.ds(0, 1), :, rows, :]),
            ("ground", (GROUND_UP, GROUND_DN), lambda rows: planes.at[pl.ds(1, 2), :, rows, :]),
        ):
            if name not in ("metric", "ground") or outer == 0:
                msg[name] = same(kinds, ref)
                msg[name + "_up"], msg[name + "_dn"] = msg[name][:1], msg[name][1:]
        return msg

    def start(copies):
        for copy in copies:
            copy.start()

    def arrive(copies):
        for copy in copies:
            copy.wait_recv()

    def sent(copies):
        for copy in copies:
            copy.wait_send()

    def tiles(count, body, unroll=1):
        def one(index, carry):
            body(index)
            return carry

        lax.fori_loop(0, count, one, 0, unroll=unroll)

    def sum_layers(outer):
        def body(tile):
            rows = pl.ds(OWN + SUB * tile, SUB)
            acc = jnp.abs(state[outer, 2, 0, mine, rows, :]) + jnp.abs(shared[outer, 0, :, rows, :])
            for layer in range(1, layers):
                acc = acc + (jnp.abs(state[outer, 2, layer, mine, rows, :]) + jnp.abs(shared[outer, layer, :, rows, :]))
            total[outer, :, rows, :] = acc

        tiles(2, body, 2)

    def weigh(outer, starts, keep_sum):
        base, stride = starts
        chip_layer = first_layer - odd * layers

        def body(tile):
            rows = pl.ds(base + stride * tile, SUB)
            running = jnp.where(is_low, above[outer, :, rows, :], 0.0)
            ours = [state[outer, 2, layer, mine, rows, :] for layer in range(layers)]
            others = [shared[outer, layer, :, rows, :] for layer in range(layers)]
            column = [jnp.where(is_even, a, b) for a, b in zip(ours, others)]
            column += [jnp.where(is_even, b, a) for a, b in zip(ours, others)]
            sums = []
            for layer, mass in enumerate(column):
                running = running + jnp.abs(mass)
                pressure = top_pressure + running * (1.0 / levels)
                sums.append(theta[chip_layer + layer] * jnp.exp(exner_power * jnp.log(pressure)))
            for layer in range(2 * layers - 2, -1, -1):
                sums[layer] = sums[layer] + sums[layer + 1]
            for layer in range(layers):
                upper, lower = sums[layer], sums[layer + layers]
                weight[outer, layer, mine, rows, :] = jnp.where(is_even, upper, lower)
                given[outer, layer, :, rows, :] = jnp.where(is_even, lower, upper)
            if keep_sum:
                exner[outer, :, rows, :] = sums[0] + planes[1, mine, rows, :]

        tiles(2, body)

    def coefficients(starts):
        base, stride = starts
        shape = (blocks, SUB, LANES)
        column = LANES * lax.broadcasted_iota(jnp.int32, shape, 0) + lax.broadcasted_iota(jnp.int32, shape, 2)
        coriolis = 0.5 + column.astype(jnp.float32) / columns

        def body(tile):
            rows = pl.ds(base + stride * tile, SUB)
            metric = planes[0, :, rows, :]
            count = planes[2, :, rows, :]
            inverse[:, rows, :] = 1.0 / metric
            half = 0.5 * metric
            square = half * metric
            for layer in range(layers):
                active = jnp.logical_or(count > (first_layer + layer).astype(jnp.float32), is_high)
                half_metric[layer, :, rows, :] = jnp.where(active, half, 0.0)
                half_square[layer, :, rows, :] = jnp.where(active, square, 0.0)
                spin[layer, :, rows, :] = jnp.where(active, coriolis, 0.0)

        tiles(2, body)

    def montgomery(outer, starts):
        base, stride = starts

        def body(tile):
            rows = pl.ds(base + stride * tile, SUB)
            rest = jnp.where(is_high, below[outer, :, rows, :], planes[1, :, rows, :])
            for layer in range(layers):
                potential[layer, :, rows, :] = rest + weight[outer, layer, :, rows, :]

        tiles(2, body, 2)

    def slopes(picked):
        def body(index):
            layer, tile = pick(picked, index)
            base = OWN - 4 + SUB * tile
            rows = pl.ds(base, SUB)
            half = half_metric[layer, :, rows, :]
            along = half * (
                potential[layer, :, pl.ds(base + 1, SUB), :] - potential[layer, :, pl.ds(base - 1, SUB), :]
            )
            across = half * column_gap(potential[layer, :, rows, :], edge=True)
            slope_x[layer, :, rows, :] = along
            slope_y[layer, :, rows, :] = across
            first[0, layer, :, rows, :] = first[0, layer, :, rows, :] - (time_step * SECTIONS[0]) * along
            first[1, layer, :, rows, :] = first[1, layer, :, rows, :] - (time_step * SECTIONS[0]) * across

        tiles(picked[0] * layers, body, 4 if picked[0] != 2 else 8)

    def pick(picked, index):
        count, begin, stride = picked
        return index // count, begin + stride * lax.rem(index, count)

    def section(outer, number, fields, results, picked=None):
        picked = picked or (2 if number == 2 else 3, 0, 1)
        begin = OWN if number == 2 else OWN - 4
        factor = time_step * SECTIONS[number]
        source = (state.at[outer], first, second)[number]

        def body(index):
            layer, tile = pick(picked, index)
            base = begin + SUB * tile

            def get(ref, field, shift=0):
                return ref[field, layer, :, pl.ds(base + shift, SUB), :]

            def plane(ref):
                return ref[layer, :, pl.ds(base, SUB), :]

            start_of = state.at[outer]
            half = plane(half_metric) * factor
            east, north = get(source, 0), get(source, 1)
            flow_x, flow_y = half * east, half * north

            def carried(field):
                middle = get(source, field)
                return flow_x * (get(source, field, 1) - get(source, field, -1)) + flow_y * column_gap(middle)

            if 0 in fields:
                turn = plane(spin) * factor
                push_x, push_y = turn * north, turn * east
                if number > 0:
                    push_x = push_x - plane(slope_x) * factor
                    push_y = push_y + plane(slope_y) * factor
                results(0, layer, tile)[...] = get(start_of, 0) + push_x - carried(0)
                results(1, layer, tile)[...] = get(start_of, 1) - push_y - carried(1)

                def flux(shift):
                    return get(source, 2, shift) * get(source, 0, shift) * inverse[:, pl.ds(base + shift, SUB), :]

                across = get(source, 2) * north * plane_of(inverse, base)
                results(2, layer, tile)[...] = get(start_of, 2) - factor * plane(half_square) * (
                    (flux(1) - flux(-1)) + column_gap(across)
                )
            for field in fields:
                if field > 2:
                    results(field, layer, tile)[...] = get(start_of, field) - carried(field)

        tiles(picked[0] * layers, body, 4 if picked[0] != 2 else 8)

    def plane_of(ref, base):
        return ref[:, pl.ds(base, SUB), :]

    outputs = (east_out, north_out, mass_out, one_out, two_out)

    def results_of(outer, number):
        if number < 2:
            ref = (first, second)[number]
            return lambda field, layer, tile: ref.at[field, layer, :, pl.ds(OWN - 4 + SUB * tile, SUB), :]
        if outer + 1 < OUTER:
            return lambda field, layer, tile: state.at[outer + 1, field, layer, :, pl.ds(OWN + SUB * tile, SUB), :]
        return lambda field, layer, tile: outputs[field].at[layer, :, pl.ds(SUB * tile, SUB), :]

    DYNAMICS, TRACERS = (0, 1, 2), (3, 4)

    def run(outer, number, fields, picked=None):
        section(outer, number, fields, results_of(outer, number), picked)

    middle, beside = (1, 1, 0), (2, 0, 2)

    inner = (OWN, SUB)
    outer_rows = (OWN - SUB, 3 * SUB)
    sends, high_sends, low_sends = [], [], []
    previous = None
    held_back = []
    for outer in range(OUTER):
        msg = all_messages(outer)

        def to_rows(copies, condition=None, first_step=outer == 0):
            allowed = condition
            if first_step:
                held_back.append((condition, copies))
                allowed = late if condition is None else late & condition
            if allowed is None:
                start(copies)
            else:
                pl.when(allowed)(functools.partial(start, copies))

        sends += msg["share"] + msg["share_edge"] + msg["give"] + msg["give_edge"]
        sends += msg["mass"] + msg["wind"] + msg["one"] + msg["two"]
        high_sends += msg["total_edge"] + msg["below"]
        low_sends += msg["exner_edge"]

        if outer == 0:
            for copy in loads_mass:
                copy.wait()
            meet()
            start(msg["share"])
            to_rows(msg["mass"])
            for copy in loads_planes:
                copy.wait()

            def count_up(tile):
                rows = pl.ds(OWN + SUB * tile, SUB)
                planes[2, :, rows, :] = active_raw[:, rows, :].astype(jnp.float32)

            tiles(2, count_up)
            to_rows(msg["metric_dn"])
            to_rows(msg["ground_dn"], is_low)
            sends += msg["metric"]
            low_sends += msg["ground"]
            for copy in loads_wind:
                copy.wait()
        else:
            start(msg["share"])
            to_rows(msg["mass"])

        arrive(msg["share"])

        @pl.when(is_high)
        def _():
            sum_layers(outer)
            start(msg["total"])

        to_rows(msg["total_edge"], is_high)
        to_rows(msg["wind_dn"])

        if outer == 0:
            coefficients(inner)
            for copy in loads_trace:
                copy.wait()

        @pl.when(is_low)
        def _():
            arrive(msg["total"])

        weigh(outer, inner, True)
        start(msg["give"])

        @pl.when(is_low)
        def _():
            start(msg["exner"])

        to_rows(msg["exner_edge"], is_low)

        @pl.when(is_high)
        def _():
            sent(msg["total"])

        if outer == 0:
            to_rows(msg["metric_up"])
            to_rows(msg["ground_up"], is_low)
        to_rows(msg["wind_up"])
        if outer > 0:
            arrive(previous["one"] + previous["two"])
            for number in range(3):
                run(outer - 1, number, TRACERS)
        to_rows(msg["one_up"] + msg["two_up"])

        if outer == 0:

            @pl.when(early)
            def _():
                pl.semaphore_wait(barrier, 6)
                for condition, copies in held_back:
                    if condition is None:
                        start(copies)
                    else:
                        pl.when(condition)(functools.partial(start, copies))

            arrive(msg["metric"])

            @pl.when(is_low)
            def _():
                arrive(msg["ground"])

            coefficients(outer_rows)
        arrive(msg["mass"])
        start(msg["share_edge"])

        @pl.when(is_low)
        def _():
            sent(msg["exner"])

        @pl.when(is_high)
        def _():
            arrive(msg["exner"])
            start(msg["below"])

        start(msg["one_dn"] + msg["two_dn"])
        arrive(msg["share_edge"])

        @pl.when(is_low)
        def _():
            arrive(msg["total_edge"])

        weigh(outer, outer_rows, False)
        start(msg["give_edge"])

        run(outer, 0, DYNAMICS, middle)
        arrive(msg["give"])

        @pl.when(is_high)
        def _():
            arrive(msg["below"])

        montgomery(outer, inner)
        slopes(middle)
        arrive(msg["wind"])
        run(outer, 0, DYNAMICS, beside)
        arrive(msg["give_edge"])

        @pl.when(is_high)
        def _():
            arrive(msg["exner_edge"])

        montgomery(outer, outer_rows)
        slopes(beside)
        for number in (1, 2):
            run(outer, number, DYNAMICS)
        previous = msg

    run(OUTER - 1, 0, TRACERS, middle)
    arrive(previous["one"] + previous["two"])
    run(OUTER - 1, 0, TRACERS, beside)
    for number in (1, 2):
        run(OUTER - 1, number, TRACERS)

    sent(sends)
    for condition, copies in (
        (is_high, high_sends),
        (is_low, low_sends),
    ):

        @pl.when(condition)
        def _(copies=copies):
            sent(copies)


def store_kernel(*refs):
    count = (len(refs) - 1) // 2
    sem = refs[-1]
    copies = [
        pltpu.make_async_copy(
            refs[field].at[:, :, pl.ds(SUB * half, SUB), :], refs[count + field].at[:, half], sem.at[field, half]
        )
        for field in range(count)
        for half in range(2)
    ]
    for copy in copies:
        copy.start()
    for copy in copies:
        copy.wait()


def local(row_devices, levels, *arguments):
    fields, theta, maps = arguments[:5], arguments[5], arguments[6:]
    layers, rows, columns = fields[0].shape
    blocks = columns // LANES

    def cut(values):
        lead = values.shape[:-2]
        values = values.reshape(lead + (rows // SUB, SUB, blocks, LANES))
        return pltpu.with_memory_space_constraint(jnp.swapaxes(values, -3, -2), pltpu.HBM)

    def joined(values):
        return jnp.swapaxes(values, -3, -2).reshape(layers, rows, columns)

    anywhere = pl.BlockSpec(memory_space=pltpu.HBM)
    in_vmem = pl.BlockSpec(memory_space=VMEM)
    part = jax.ShapeDtypeStruct((layers, blocks, rows, LANES), jnp.float32)
    half_plane = VMEM((OUTER, blocks // 2, DEPTH, LANES), jnp.float32)
    volume = VMEM((layers, blocks, DEPTH, LANES), jnp.float32)
    results = pl.pallas_call(
        functools.partial(steps_kernel, levels, columns, row_devices, PERIOD),
        name="layer_steps",
        out_shape=[part] * 5,
        in_specs=[anywhere] * 5 + [pl.BlockSpec(memory_space=pltpu.SMEM)] + [anywhere] * 3,
        out_specs=[in_vmem] * 5,
        scratch_shapes=[
            VMEM((OUTER, 5, layers, blocks, DEPTH, LANES), jnp.float32),
            VMEM((5, layers, blocks, DEPTH, LANES), jnp.float32),
            VMEM((5, layers, blocks, DEPTH, LANES), jnp.float32),
            VMEM((3, blocks, DEPTH, LANES), jnp.float32),
            VMEM((blocks, DEPTH, LANES), jnp.int32),
        ]
        + [half_plane] * 3
        + [VMEM((OUTER, blocks, DEPTH, LANES), jnp.float32)]
        + [VMEM((OUTER, layers, blocks // 2, DEPTH, LANES), jnp.float32)] * 2
        + [VMEM((OUTER, layers, blocks, DEPTH, LANES), jnp.float32)]
        + [volume] * 6
        + [
            VMEM((blocks, DEPTH, LANES), jnp.float32),
            pltpu.SemaphoreType.DMA((8, 2)),
            pltpu.SemaphoreType.DMA((OUTER, MESSAGES)),
            pltpu.SemaphoreType.DMA((OUTER, MESSAGES)),
        ],
        compiler_params=pltpu.CompilerParams(
            collective_id=0, has_side_effects=True, vmem_limit_bytes=48 * 2**20
        ),
    )(*[cut(values) for values in fields], pltpu.with_memory_space_constraint(theta, pltpu.HBM), *[cut(values) for values in maps])

    stored = pl.pallas_call(
        store_kernel,
        name="store_layers",
        out_shape=[jax.ShapeDtypeStruct((layers, rows // SUB, blocks, SUB, LANES), jnp.float32)] * 5,
        in_specs=[in_vmem] * 5,
        out_specs=[anywhere] * 5,
        scratch_shapes=[pltpu.SemaphoreType.DMA((5, 2))],
        compiler_params=pltpu.CompilerParams(vmem_limit_bytes=2**20),
    )(*results)
    return tuple(joined(values) for values in stored)


def solution(mesh):
    layered = P("lev", "row", None)
    flat = P("row", None)
    row_devices, lev_devices = mesh.shape["row"], mesh.shape["lev"]

    def whole(*arguments):
        levels = arguments[0].shape[0]
        return jax.shard_map(
            functools.partial(local, row_devices, levels),
            mesh=mesh,
            in_specs=(layered,) * 5 + (P(),) + (flat,) * 3,
            out_specs=(layered,) * 5,
            check_vma=False,
        )(*arguments)

    return whole
```

```python
import functools

import jax
import jax.numpy as jnp
from jax import lax
from jax.experimental import pallas as pl
from jax.experimental.pallas import tpu as pltpu
from jax.sharding import PartitionSpec as P

OUTER = 2
SECTIONS = (1.0 / 3.0, 0.5, 1.0)

time_step = 0.05
top_pressure = 0.1
exner_power = 2.0 / 7.0

MESH = pl.DeviceIdType.MESH
VMEM = pltpu.VMEM

PERIOD = 64
HALO = 3
OWN = 12
DEPTH = 40
LANES = 128
SUB = 8

SHARE, SHARE_LOW, SHARE_HIGH, TOTAL, TOTAL_UP, TOTAL_DN = range(6)
EXNER, EXNER_UP, EXNER_DN, GIVE, GIVE_LOW, GIVE_HIGH, BELOW, CROSS_UP, CROSS_DN = range(6, 15)
MASS_UP, MASS_DN, WIND_UP, WIND_DN, ONE_UP, ONE_DN, TWO_UP, TWO_DN = range(15, 23)
METRIC_UP, METRIC_DN, GROUND_UP, GROUND_DN = range(23, 27)
MESSAGES = 27


def column_gap(a, edge=False):
    lane = lax.broadcasted_iota(jnp.int32, (1,) + a.shape[1:], 2)
    low, high = (a[:1], a[-1:]) if edge else (jnp.zeros_like(a[:1]), jnp.zeros_like(a[:1]))
    east = pltpu.roll(a, LANES - 1, 2)
    west = pltpu.roll(a, 1, 2)
    east = jnp.where(lane == LANES - 1, jnp.concatenate([east[1:], high], 0), east)
    west = jnp.where(lane == 0, jnp.concatenate([low, west[:-1]], 0), west)
    return east - west


def steps_kernel(
    levels,
    columns,
    row_devices,
    period,
    east_in,
    north_in,
    mass_in,
    one_in,
    two_in,
    theta,
    geopot_in,
    metric_in,
    active_in,
    east_out,
    north_out,
    mass_out,
    one_out,
    two_out,
    state,
    first,
    second,
    planes,
    active_raw,
    total,
    above,
    exner,
    below,
    shared,
    given,
    weight,
    potential,
    slope_x,
    slope_y,
    half_metric,
    half_square,
    spin,
    inverse,
    load_sem,
    send_sem,
    recv_sem,
):
    layers, blocks = state.shape[2], state.shape[3]
    lev, row = lax.axis_index("lev"), lax.axis_index("row")
    up_row = lax.rem(row + 1, row_devices)
    dn_row = lax.rem(row + row_devices - 1, row_devices)
    odd = lax.rem(lev, 2)
    core = (lev + 1 - 2 * odd, row)
    far_lev = lax.rem(lev + 2, 4)
    far, far_up, far_dn = (far_lev, row), (far_lev, up_row), (far_lev, dn_row)
    up, dn = (lev, up_row), (lev, dn_row)
    cross_lev = far_lev + 1 - 2 * odd
    cross_up, cross_dn = (cross_lev, up_row), (cross_lev, dn_row)
    is_even = odd == 0
    half_blocks = blocks // 2
    mine = pl.ds(odd * half_blocks, half_blocks)
    theirs = pl.ds((1 - odd) * half_blocks, half_blocks)
    is_high, is_low = lev < 2, lev >= 2
    own = pl.ds(OWN, 2 * SUB)
    first_layer = lev * layers

    def load(slot, source, target):
        return [
            pltpu.make_async_copy(
                source(half), target(pl.ds(OWN + half * SUB, SUB)), load_sem.at[slot, half]
            )
            for half in range(2)
        ]

    def load_field(slot, ref, field):
        return load(slot, lambda half: ref.at[:, half], lambda rows: state.at[0, field, :, :, rows, :])

    loads_mass = load_field(0, mass_in, 2)
    loads_planes = (
        load(1, lambda half: metric_in.at[half], lambda rows: planes.at[0, :, rows, :])
        + load(2, lambda half: geopot_in.at[half], lambda rows: planes.at[1, :, rows, :])
        + load(3, lambda half: active_in.at[half], lambda rows: active_raw.at[:, rows, :])
    )
    loads_wind = load_field(4, east_in, 0) + load_field(5, north_in, 1)
    loads_trace = load_field(6, one_in, 3) + load_field(7, two_in, 4)
    for copy in loads_mass + loads_planes + loads_wind + loads_trace:
        copy.start()

    early = lax.rem(row, period) == 0
    late = jnp.logical_not(early)
    up_early, dn_early = lax.rem(up_row, period) == 0, lax.rem(dn_row, period) == 0
    barrier = pltpu.get_barrier_semaphore()

    def greet(*devices):
        for device in devices:
            pl.semaphore_signal(barrier, inc=1, device_id=device, device_id_type=MESH)

    greet(core, far)

    @pl.when(late & jnp.logical_not(up_early))
    def _():
        greet(up, far_up, cross_up)

    @pl.when(late & jnp.logical_not(dn_early))
    def _():
        greet(dn, far_dn, cross_dn)

    def meet():
        @pl.when(early)
        def _():
            pl.semaphore_wait(barrier, 2)
            greet(up, far_up, cross_up, dn, far_dn, cross_dn)

        @pl.when(late)
        def _():
            pl.semaphore_wait(barrier, 8)

        @pl.when(late & up_early)
        def _():
            greet(up, far_up, cross_up)

        @pl.when(late & dn_early)
        def _():
            greet(dn, far_dn, cross_dn)

    def message(outer, kind, source, target, device):
        return pltpu.make_async_remote_copy(
            src_ref=source,
            dst_ref=target,
            send_sem=send_sem.at[outer, kind],
            recv_sem=recv_sem.at[outer, kind],
            device_id=device,
            device_id_type=MESH,
        )

    edge_up = (pl.ds(OWN + 2 * SUB - HALO, HALO), pl.ds(OWN - HALO, HALO))
    edge_dn = (pl.ds(OWN, HALO), pl.ds(OWN + 2 * SUB, HALO))

    def edges(outer, kinds, ref, ref_to, to_up, to_dn):
        return [
            message(outer, kind, ref(rows[0]), ref_to(rows[1]), device)
            for kind, rows, device in zip(kinds, (edge_up, edge_dn), (to_up, to_dn))
        ]

    def plane_rows(ref, outer):
        return lambda rows: ref.at[outer, :, rows, :]

    def field_rows(outer, field, count):
        return lambda rows: state.at[outer, pl.ds(field, count), :, :, rows, :]

    def all_messages(outer):
        same = lambda kinds, ref: edges(outer, kinds, ref, ref, up, dn)
        msg = {}
        low_rows, high_rows = edge_up[1], edge_dn[1]

        def to_core(kinds, ref, ref_to):
            return [
                message(outer, kind, ref(rows), ref_to(rows), core)
                for kind, rows in zip(kinds, (own, low_rows, high_rows))
            ]

        half_below = lambda rows: below.at[outer, mine, rows, :]
        for name, copies in (
            (
                "share",
                to_core(
                    (SHARE, SHARE_LOW, SHARE_HIGH),
                    lambda rows: state.at[outer, 2, :, theirs, rows, :],
                    lambda rows: shared.at[outer, :, :, rows, :],
                ),
            ),
            (
                "give",
                to_core(
                    (GIVE, GIVE_LOW, GIVE_HIGH),
                    lambda rows: given.at[outer, :, :, rows, :],
                    lambda rows: weight.at[outer, :, mine, rows, :],
                ),
            ),
        ):
            msg[name], msg[name + "_edge"] = copies[:1], copies[1:]
        msg["total"] = [message(outer, TOTAL, total.at[outer, :, own, :], above.at[outer, :, own, :], far)]
        msg["total_edge"] = edges(
            outer, (TOTAL_UP, TOTAL_DN), plane_rows(total, outer), plane_rows(above, outer), far_up, far_dn
        )
        msg["exner"] = [message(outer, EXNER, exner.at[outer, :, own, :], half_below(own), far)]
        msg["below"] = [message(outer, BELOW, half_below(own), half_below(own), core)]
        msg["exner_edge"] = edges(
            outer, (EXNER_UP, EXNER_DN), plane_rows(exner, outer), half_below, far_up, far_dn
        ) + edges(outer, (CROSS_UP, CROSS_DN), plane_rows(exner, outer), half_below, cross_up, cross_dn)
        for name, kinds, ref in (
            ("mass", (MASS_UP, MASS_DN), field_rows(outer, 2, 1)),
            ("wind", (WIND_UP, WIND_DN), field_rows(outer, 0, 2)),
            ("one", (ONE_UP, ONE_DN), field_rows(outer, 3, 1)),
            ("two", (TWO_UP, TWO_DN), field_rows(outer, 4, 1)),
            ("metric", (METRIC_UP, METRIC_DN), lambda rows: planes.at[pl.ds(0, 1), :, rows, :]),
            ("ground", (GROUND_UP, GROUND_DN), lambda rows: planes.at[pl.ds(1, 2), :, rows, :]),
        ):
            if name not in ("metric", "ground") or outer == 0:
                msg[name] = same(kinds, ref)
                msg[name + "_up"], msg[name + "_dn"] = msg[name][:1], msg[name][1:]
        return msg

    def start(copies):
        for copy in copies:
            copy.start()

    def arrive(copies):
        for copy in copies:
            copy.wait_recv()

    def sent(copies):
        for copy in copies:
            copy.wait_send()

    def tiles(count, body, unroll=1):
        def one(index, carry):
            body(index)
            return carry

        lax.fori_loop(0, count, one, 0, unroll=unroll)

    def sum_layers(outer):
        def body(tile):
            rows = pl.ds(OWN + SUB * tile, SUB)
            acc = jnp.abs(state[outer, 2, 0, mine, rows, :]) + jnp.abs(shared[outer, 0, :, rows, :])
            for layer in range(1, layers):
                acc = acc + (jnp.abs(state[outer, 2, layer, mine, rows, :]) + jnp.abs(shared[outer, layer, :, rows, :]))
            total[outer, :, rows, :] = acc

        tiles(2, body, 2)

    def weigh(outer, starts, keep_sum):
        base, stride = starts
        chip_layer = first_layer - odd * layers

        def body(tile):
            rows = pl.ds(base + stride * tile, SUB)
            running = jnp.where(is_low, above[outer, :, rows, :], 0.0)
            ours = [state[outer, 2, layer, mine, rows, :] for layer in range(layers)]
            others = [shared[outer, layer, :, rows, :] for layer in range(layers)]
            column = [jnp.where(is_even, a, b) for a, b in zip(ours, others)]
            column += [jnp.where(is_even, b, a) for a, b in zip(ours, others)]
            sums = []
            for layer, mass in enumerate(column):
                running = running + jnp.abs(mass)
                pressure = top_pressure + running * (1.0 / levels)
                sums.append(theta[chip_layer + layer] * jnp.exp(exner_power * jnp.log(pressure)))
            for layer in range(2 * layers - 2, -1, -1):
                sums[layer] = sums[layer] + sums[layer + 1]
            for layer in range(layers):
                upper, lower = sums[layer], sums[layer + layers]
                weight[outer, layer, mine, rows, :] = jnp.where(is_even, upper, lower)
                given[outer, layer, :, rows, :] = jnp.where(is_even, lower, upper)
            if keep_sum:
                exner[outer, :, rows, :] = sums[0] + planes[1, mine, rows, :]

        tiles(2, body, 2)

    def coefficients(starts):
        base, stride = starts
        shape = (blocks, SUB, LANES)
        column = LANES * lax.broadcasted_iota(jnp.int32, shape, 0) + lax.broadcasted_iota(jnp.int32, shape, 2)
        coriolis = 0.5 + column.astype(jnp.float32) / columns

        def body(tile):
            rows = pl.ds(base + stride * tile, SUB)
            metric = planes[0, :, rows, :]
            count = planes[2, :, rows, :]
            inverse[:, rows, :] = 1.0 / metric
            half = 0.5 * metric
            square = half * metric
            for layer in range(layers):
                active = jnp.logical_or(count > (first_layer + layer).astype(jnp.float32), is_high)
                half_metric[layer, :, rows, :] = jnp.where(active, half, 0.0)
                half_square[layer, :, rows, :] = jnp.where(active, square, 0.0)
                spin[layer, :, rows, :] = jnp.where(active, coriolis, 0.0)

        tiles(2, body)

    def montgomery(outer, starts):
        base, stride = starts

        def body(tile):
            rows = pl.ds(base + stride * tile, SUB)
            rest = jnp.where(is_high, below[outer, :, rows, :], planes[1, :, rows, :])
            for layer in range(layers):
                potential[layer, :, rows, :] = rest + weight[outer, layer, :, rows, :]

        tiles(2, body, 2)

    def slopes(picked):
        def body(index):
            layer, tile = pick(picked, index)
            base = OWN - 4 + SUB * tile
            rows = pl.ds(base, SUB)
            half = half_metric[layer, :, rows, :]
            along = half * (
                potential[layer, :, pl.ds(base + 1, SUB), :] - potential[layer, :, pl.ds(base - 1, SUB), :]
            )
            across = half * column_gap(potential[layer, :, rows, :], edge=True)
            slope_x[layer, :, rows, :] = along
            slope_y[layer, :, rows, :] = across
            first[0, layer, :, rows, :] = first[0, layer, :, rows, :] - (time_step * SECTIONS[0]) * along
            first[1, layer, :, rows, :] = first[1, layer, :, rows, :] - (time_step * SECTIONS[0]) * across

        tiles(picked[0] * layers, body, 4 if picked[0] != 2 else 8)

    def pick(picked, index):
        count, begin, stride = picked
        return index // count, begin + stride * lax.rem(index, count)

    def section(outer, number, fields, results, picked=None):
        picked = picked or (2 if number == 2 else 3, 0, 1)
        begin = OWN if number == 2 else OWN - 4
        factor = time_step * SECTIONS[number]
        source = (state.at[outer], first, second)[number]

        def body(index):
            layer, tile = pick(picked, index)
            base = begin + SUB * tile

            def get(ref, field, shift=0):
                return ref[field, layer, :, pl.ds(base + shift, SUB), :]

            def plane(ref):
                return ref[layer, :, pl.ds(base, SUB), :]

            start_of = state.at[outer]
            half = plane(half_metric) * factor
            east, north = get(source, 0), get(source, 1)
            flow_x, flow_y = half * east, half * north

            def carried(field):
                middle = get(source, field)
                return flow_x * (get(source, field, 1) - get(source, field, -1)) + flow_y * column_gap(middle)

            if 0 in fields:
                turn = plane(spin) * factor
                push_x, push_y = turn * north, turn * east
                if number > 0:
                    push_x = push_x - plane(slope_x) * factor
                    push_y = push_y + plane(slope_y) * factor
                results(0, layer, tile)[...] = get(start_of, 0) + push_x - carried(0)
                results(1, layer, tile)[...] = get(start_of, 1) - push_y - carried(1)

                def flux(shift):
                    return get(source, 2, shift) * get(source, 0, shift) * inverse[:, pl.ds(base + shift, SUB), :]

                across = get(source, 2) * north * plane_of(inverse, base)
                results(2, layer, tile)[...] = get(start_of, 2) - factor * plane(half_square) * (
                    (flux(1) - flux(-1)) + column_gap(across)
                )
            for field in fields:
                if field > 2:
                    results(field, layer, tile)[...] = get(start_of, field) - carried(field)

        tiles(picked[0] * layers, body, 4 if picked[0] != 2 else 8)

    def plane_of(ref, base):
        return ref[:, pl.ds(base, SUB), :]

    outputs = (east_out, north_out, mass_out, one_out, two_out)

    def results_of(outer, number):
        if number < 2:
            ref = (first, second)[number]
            return lambda field, layer, tile: ref.at[field, layer, :, pl.ds(OWN - 4 + SUB * tile, SUB), :]
        if outer + 1 < OUTER:
            return lambda field, layer, tile: state.at[outer + 1, field, layer, :, pl.ds(OWN + SUB * tile, SUB), :]
        return lambda field, layer, tile: outputs[field].at[layer, :, pl.ds(SUB * tile, SUB), :]

    DYNAMICS, TRACERS = (0, 1, 2), (3, 4)

    def run(outer, number, fields, picked=None):
        section(outer, number, fields, results_of(outer, number), picked)

    middle, beside = (1, 1, 0), (2, 0, 2)

    inner = (OWN, SUB)
    outer_rows = (OWN - SUB, 3 * SUB)
    sends, high_sends, low_sends = [], [], []
    previous = None
    held_back = []
    for outer in range(OUTER):
        msg = all_messages(outer)

        def to_rows(copies, condition=None, first_step=outer == 0):
            allowed = condition
            if first_step:
                held_back.append((condition, copies))
                allowed = late if condition is None else late & condition
            if allowed is None:
                start(copies)
            else:
                pl.when(allowed)(functools.partial(start, copies))

        sends += msg["share"] + msg["share_edge"] + msg["give"] + msg["give_edge"]
        sends += msg["mass"] + msg["wind"] + msg["one"] + msg["two"]
        high_sends += msg["total_edge"] + msg["below"]
        low_sends += msg["exner_edge"]

        if outer == 0:
            for copy in loads_mass:
                copy.wait()
            meet()
            start(msg["share"])
            to_rows(msg["mass"])
            for copy in loads_planes:
                copy.wait()

            def count_up(tile):
                rows = pl.ds(OWN + SUB * tile, SUB)
                planes[2, :, rows, :] = active_raw[:, rows, :].astype(jnp.float32)

            tiles(2, count_up)
            to_rows(msg["metric_dn"])
            to_rows(msg["ground_dn"], is_low)
            sends += msg["metric"]
            low_sends += msg["ground"]
            for copy in loads_wind:
                copy.wait()
        else:
            start(msg["share"])
            to_rows(msg["mass"])

        arrive(msg["share"])

        @pl.when(is_high)
        def _():
            sum_layers(outer)
            start(msg["total"])

        to_rows(msg["total_edge"], is_high)
        to_rows(msg["wind_dn"])

        if outer == 0:
            coefficients(inner)
            for copy in loads_trace:
                copy.wait()

        @pl.when(is_low)
        def _():
            arrive(msg["total"])

        weigh(outer, inner, True)

        @pl.when(is_low)
        def _():
            start(msg["exner"])

        to_rows(msg["exner_edge"], is_low)
        start(msg["give"])

        @pl.when(is_high)
        def _():
            sent(msg["total"])

        if outer == 0:
            to_rows(msg["metric_up"])
            to_rows(msg["ground_up"], is_low)
        to_rows(msg["wind_up"])
        if outer > 0:
            arrive(previous["one"] + previous["two"])
            for number in range(3):
                run(outer - 1, number, TRACERS)
        to_rows(msg["one_up"] + msg["two_up"])

        if outer == 0:

            @pl.when(early)
            def _():
                pl.semaphore_wait(barrier, 6)
                for condition, copies in held_back:
                    if condition is None:
                        start(copies)
                    else:
                        pl.when(condition)(functools.partial(start, copies))

            arrive(msg["metric"])

            @pl.when(is_low)
            def _():
                arrive(msg["ground"])

            coefficients(outer_rows)
        arrive(msg["mass"])
        start(msg["share_edge"])

        @pl.when(is_low)
        def _():
            sent(msg["exner"])

        @pl.when(is_high)
        def _():
            arrive(msg["exner"])
            start(msg["below"])

        start(msg["one_dn"] + msg["two_dn"])
        arrive(msg["share_edge"])

        @pl.when(is_low)
        def _():
            arrive(msg["total_edge"])

        weigh(outer, outer_rows, False)
        start(msg["give_edge"])

        run(outer, 0, DYNAMICS, middle)
        arrive(msg["give"])

        @pl.when(is_high)
        def _():
            arrive(msg["below"])

        montgomery(outer, inner)
        slopes(middle)
        arrive(msg["wind"])
        run(outer, 0, DYNAMICS, beside)
        arrive(msg["give_edge"])

        @pl.when(is_high)
        def _():
            arrive(msg["exner_edge"])

        montgomery(outer, outer_rows)
        slopes(beside)
        for number in (1, 2):
            run(outer, number, DYNAMICS)
        previous = msg

    run(OUTER - 1, 0, TRACERS, middle)
    arrive(previous["one"] + previous["two"])
    run(OUTER - 1, 0, TRACERS, beside)
    for number in (1, 2):
        run(OUTER - 1, number, TRACERS)

    sent(sends)
    for condition, copies in (
        (is_high, high_sends),
        (is_low, low_sends),
    ):

        @pl.when(condition)
        def _(copies=copies):
            sent(copies)


def store_kernel(*refs):
    count = (len(refs) - 1) // 2
    sem = refs[-1]
    copies = [
        pltpu.make_async_copy(
            refs[field].at[:, :, pl.ds(SUB * half, SUB), :], refs[count + field].at[:, half], sem.at[field, half]
        )
        for field in range(count)
        for half in range(2)
    ]
    for copy in copies:
        copy.start()
    for copy in copies:
        copy.wait()


def local(row_devices, levels, *arguments):
    fields, theta, maps = arguments[:5], arguments[5], arguments[6:]
    layers, rows, columns = fields[0].shape
    blocks = columns // LANES

    def cut(values):
        lead = values.shape[:-2]
        values = values.reshape(lead + (rows // SUB, SUB, blocks, LANES))
        return pltpu.with_memory_space_constraint(jnp.swapaxes(values, -3, -2), pltpu.HBM)

    def joined(values):
        return jnp.swapaxes(values, -3, -2).reshape(layers, rows, columns)

    anywhere = pl.BlockSpec(memory_space=pltpu.HBM)
    in_vmem = pl.BlockSpec(memory_space=VMEM)
    part = jax.ShapeDtypeStruct((layers, blocks, rows, LANES), jnp.float32)
    half_plane = VMEM((OUTER, blocks // 2, DEPTH, LANES), jnp.float32)
    volume = VMEM((layers, blocks, DEPTH, LANES), jnp.float32)
    results = pl.pallas_call(
        functools.partial(steps_kernel, levels, columns, row_devices, PERIOD),
        name="layer_steps",
        out_shape=[part] * 5,
        in_specs=[anywhere] * 5 + [pl.BlockSpec(memory_space=pltpu.SMEM)] + [anywhere] * 3,
        out_specs=[in_vmem] * 5,
        scratch_shapes=[
            VMEM((OUTER, 5, layers, blocks, DEPTH, LANES), jnp.float32),
            VMEM((5, layers, blocks, DEPTH, LANES), jnp.float32),
            VMEM((5, layers, blocks, DEPTH, LANES), jnp.float32),
            VMEM((3, blocks, DEPTH, LANES), jnp.float32),
            VMEM((blocks, DEPTH, LANES), jnp.int32),
        ]
        + [half_plane] * 3
        + [VMEM((OUTER, blocks, DEPTH, LANES), jnp.float32)]
        + [VMEM((OUTER, layers, blocks // 2, DEPTH, LANES), jnp.float32)] * 2
        + [VMEM((OUTER, layers, blocks, DEPTH, LANES), jnp.float32)]
        + [volume] * 6
        + [
            VMEM((blocks, DEPTH, LANES), jnp.float32),
            pltpu.SemaphoreType.DMA((8, 2)),
            pltpu.SemaphoreType.DMA((OUTER, MESSAGES)),
            pltpu.SemaphoreType.DMA((OUTER, MESSAGES)),
        ],
        compiler_params=pltpu.CompilerParams(
            collective_id=0, has_side_effects=True, vmem_limit_bytes=48 * 2**20
        ),
    )(*[cut(values) for values in fields], pltpu.with_memory_space_constraint(theta, pltpu.HBM), *[cut(values) for values in maps])

    stored = pl.pallas_call(
        store_kernel,
        name="store_layers",
        out_shape=[jax.ShapeDtypeStruct((layers, rows // SUB, blocks, SUB, LANES), jnp.float32)] * 5,
        in_specs=[in_vmem] * 5,
        out_specs=[anywhere] * 5,
        scratch_shapes=[pltpu.SemaphoreType.DMA((5, 2))],
        compiler_params=pltpu.CompilerParams(vmem_limit_bytes=2**20),
    )(*results)
    return tuple(joined(values) for values in stored)


def solution(mesh):
    layered = P("lev", "row", None)
    flat = P("row", None)
    row_devices, lev_devices = mesh.shape["row"], mesh.shape["lev"]

    def whole(*arguments):
        levels = arguments[0].shape[0]
        return jax.shard_map(
            functools.partial(local, row_devices, levels),
            mesh=mesh,
            in_specs=(layered,) * 5 + (P(),) + (flat,) * 3,
            out_specs=(layered,) * 5,
            check_vma=False,
        )(*arguments)

    return whole
```
